32 devices in a mesh: blk: 16 (over z, y, core), col: 2 (over x).
Axes of the slice: x: 2, y: 2, z: 4, core: 2. Of those that a mesh axis runs over, the one named last changes fastest.
Arguments:
- node_feats: bfloat16 [256, 32768], P('col', 'blk'), may hold values from -6 to 6
- tile_dst: int32 [896], P('blk'), may hold values from 0 to 15
- tile_src: int32 [896], P('blk'), may hold values from 0 to 47, as said below
- tile_cnt: int32 [896, 128, 128], P('blk'), may hold values from 0 to 3, as said below
- send_blk: int32 [16, 8, 4], P('blk'), may hold values from 0 to 15
- self_weight: bfloat16 [256, 256], replicated, may hold values from -0.375 to 0.375
- neigh_weight: bfloat16 [256, 256], replicated, may hold values from -0.75 to 0.75
- bias: float32 [256], replicated, may hold values from -4 to 4
- cotangent: bfloat16 [256, 32768], P('col', 'blk'), may hold values from -6 to 6
Outputs:
- grad_feats: bfloat16 [256, 32768], P('col', 'blk')
- grad_self: float32 [256, 256], P('col')
- grad_neigh: float32 [256, 256], P('col')
- grad_bias: float32 [256], P('col')
The draws below stay inside these ranges and needn't reach their ends.
Inputs may be any that keep to these rules, and one draw needn't show every extreme that they name: `tile_src`: of each device's 56 entries, the first 32 are 16 + a permutation of 0 to 32 - 1 (every received slot is read by one tile); the others are own blocks below 16. `tile_cnt`: edge counts; some rows of a tile are empty.
All inputs are finite; a program needn't handle non-finite values.
Results may differ from the reference program's by a relative error of at most 0.006.
Values may be sent and summed in bfloat16 or wider, within the bound.
A program may use at most 64 MiB of HBM per device.

```python
import jax
import jax.numpy as jnp
from jax import lax

D = 256
BLK = 128
HOPS = 4
NB_DEV = 16
SCAP = 4
LOCAL_TILES = 24
SLOTS = 32
TILES = 56
NODES = 32768
N_BLK = 16


def draw_tile_dst(key, part):
    table = jax.random.randint(key, (N_BLK, TILES), 0, NB_DEV, dtype=jnp.int32)
    table = table.at[:, 0].set(NB_DEV - 1)
    table = table.at[:, 1].set(0)
    return table.reshape(N_BLK * TILES)


def draw_tile_src(key, part):
    perm_key, local_key = jax.random.split(jax.random.fold_in(key, 11))
    keys = jax.random.split(perm_key, N_BLK)
    orders = jax.vmap(lambda single: jax.random.permutation(single, SLOTS))(keys).astype(jnp.int32)
    local_part = jax.random.randint(local_key, (N_BLK, LOCAL_TILES), 0, NB_DEV, dtype=jnp.int32)
    local_part = local_part.at[:, 0].set(0)
    table = jnp.concatenate([orders + NB_DEV, local_part], axis=1)
    return table.reshape(N_BLK * TILES)


def draw_tile_cnt(key, part):
    row_key, entry_key, value_key = jax.random.split(jax.random.fold_in(key, 23), 3)
    total = N_BLK * TILES
    active = jax.random.randint(row_key, (total, BLK, 1), 0, 2, dtype=jnp.int32)
    present = (jax.random.randint(entry_key, (total, BLK, BLK), 0, 16, dtype=jnp.int32) == 0).astype(jnp.int32)
    values = jax.random.randint(value_key, (total, BLK, BLK), 1, 4, dtype=jnp.int32)
    counts = active * present * values
    return counts.at[0, 0, 0].set(3)


def place_ends(values, stream_key, low, high):
    longest = values.shape.index(max(values.shape))
    spots = []
    for shift in (0, 1):
        where = [jax.random.randint(jax.random.fold_in(stream_key, axis), (), 0, length) for axis, length in enumerate(values.shape)]
        where[longest] = (where[longest] + shift) % values.shape[longest]
        spots.append(tuple(where))
    return values.at[spots[0]].set(low).at[spots[1]].set(high)


def steps_of(stream_key, dims, cuts, smallest, high):
    level, own = 1.0, jax.random.fold_in(stream_key, 6)
    for axis_at, parts in cuts:
        draws = jnp.exp(jax.random.uniform(jax.random.fold_in(own, axis_at), (parts,), jnp.float32, smallest / len(cuts), high / len(cuts)))
        level = level * jnp.repeat(draws, dims[axis_at] // parts).reshape([-1 if axis == axis_at else 1 for axis in range(len(dims))])
    return level


def scatter_about(key, shape, spread, bound, shards=(), kind=jnp.bfloat16):
    result = jax.random.normal(key, shape, jnp.float32) * spread
    if len(shards) > 0:
        result = steps_of(key, shape, shards, -0.22, 0.18) * result
    return jnp.clip(result, min=-bound, max=bound).astype(kind)


def setup_inputs(seed: int = 0) -> dict:
    arg_keys = jax.random.split(jax.random.key(seed), 10)
    return {
        "node_feats": scatter_about(arg_keys[0], (D, NODES), 1.0, 6.0, ((0, 2), (1, 16))),
        "tile_dst": draw_tile_dst(jax.random.fold_in(arg_keys[9], 71), 0),
        "tile_src": draw_tile_src(jax.random.fold_in(arg_keys[9], 71), 0),
        "tile_cnt": draw_tile_cnt(jax.random.fold_in(arg_keys[9], 71), 0),
        "send_blk": place_ends(jax.random.randint(arg_keys[4], (N_BLK, 2 * HOPS, SCAP), 0, NB_DEV), jax.random.fold_in(arg_keys[4], 1), 0, NB_DEV - 1).astype(jnp.int32),
        "self_weight": scatter_about(arg_keys[5], (D, D), D ** -0.5, 0.375),
        "neigh_weight": scatter_about(arg_keys[6], (D, D), (D // 4) ** -0.5, 0.75),
        "bias": scatter_about(arg_keys[7], (D,), 0.7, 4.0, (), jnp.float32),
        "cotangent": scatter_about(arg_keys[8], (D, NODES), 1.0, 6.0, ((0, 2), (1, 16))),
    }


def gelu_slope(pre_act):
    inner = 0.7978845608 * (pre_act + 0.044715 * pre_act * pre_act * pre_act)
    tanh_value = jnp.tanh(inner)
    return 0.5 * (1.0 + tanh_value) + 0.5 * pre_act * (1.0 - tanh_value * tanh_value) * 0.7978845608 * (1.0 + 3.0 * 0.044715 * pre_act * pre_act)


def reference(node_feats, tile_dst, tile_src, tile_cnt, send_blk, self_weight, neigh_weight, bias, cotangent):
    width = node_feats.shape[0]
    all_blocks = N_BLK * NB_DEV
    highest = lax.Precision.HIGHEST
    feat_blocks = node_feats.astype(jnp.float32).reshape(width, all_blocks, BLK)
    dest_table = tile_dst.reshape(N_BLK, TILES)
    source_table = tile_src.reshape(N_BLK, TILES)
    counts = tile_cnt.reshape(N_BLK, TILES, BLK, BLK)
    device_ids = jnp.arange(N_BLK, dtype=jnp.int32)[:, None]
    is_local = source_table < NB_DEV
    remote_index = jnp.maximum(source_table - NB_DEV, 0)
    offset_index = remote_index // SCAP
    slot_index = remote_index % SCAP
    distance = (offset_index // 2 + 1) * (1 - 2 * (offset_index % 2))
    sender = (device_ids - distance) % N_BLK
    sent_block = send_blk[sender, offset_index, slot_index]
    global_src = jnp.where(is_local, device_ids * NB_DEV + source_table, sender * NB_DEV + sent_block).astype(jnp.int32)
    dest_onehot = (dest_table[:, :, None] == jnp.arange(NB_DEV, dtype=jnp.int32)[None, None, :]).astype(jnp.float32)

    def forward_one(inputs):
        sources, tile_counts, onehot = inputs
        picked = feat_blocks[:, sources]
        count_float = tile_counts.astype(jnp.float32)
        products = jnp.einsum("ctj,tij->cti", picked, count_float, precision=highest)
        summed = jnp.einsum("cti,tb->cbi", products, onehot, precision=highest)
        degree_part = jnp.einsum("ti,tb->bi", jnp.sum(tile_counts, axis=2).astype(jnp.float32), onehot, precision=highest)
        return summed, degree_part

    agg_raw, degree = lax.map(forward_one, (global_src, counts, dest_onehot))
    agg_raw = agg_raw.transpose(1, 0, 2, 3).reshape(width, NODES)
    floor_degree = jnp.maximum(degree.reshape(NODES), 1.0)
    aggregate = (agg_raw / floor_degree[None, :]).astype(jnp.bfloat16)
    pre_act = (jnp.dot(self_weight.T, node_feats, preferred_element_type=jnp.float32)
               + jnp.dot(neigh_weight.T, aggregate, preferred_element_type=jnp.float32)
               + bias[:, None])
    grad_pre = (cotangent.astype(jnp.float32) * gelu_slope(pre_act)).astype(jnp.bfloat16)
    grad_self = jnp.dot(node_feats, grad_pre.T, preferred_element_type=jnp.float32)
    grad_neigh = jnp.dot(aggregate, grad_pre.T, preferred_element_type=jnp.float32)
    grad_bias = jnp.sum(grad_pre.astype(jnp.float32), axis=1)
    scaled = (jnp.dot(neigh_weight, grad_pre, preferred_element_type=jnp.float32) / floor_degree[None, :]).astype(jnp.bfloat16)
    scaled_blocks = scaled.astype(jnp.float32).reshape(width, N_BLK, NB_DEV, BLK).transpose(1, 0, 2, 3)

    def backward_one(total, inputs):
        sources, tile_counts, onehot, part = inputs
        picked = jnp.einsum("cbi,tb->cti", part, onehot, precision=highest)
        contrib = jnp.einsum("cti,tij->ctj", picked, tile_counts.astype(jnp.float32), precision=highest)
        return total.at[:, sources].add(contrib), None

    back_sum, leftover = lax.scan(backward_one, jnp.zeros((width, all_blocks, BLK), jnp.float32),
                                  (global_src, counts, dest_onehot, scaled_blocks))
    grad_feats = (jnp.dot(self_weight, grad_pre, preferred_element_type=jnp.float32)
                  + back_sum.reshape(width, NODES)).astype(jnp.bfloat16)
    return grad_feats, grad_self, grad_neigh, grad_bias
```

```python
import functools

import jax
import jax.numpy as jnp
from jax import lax
from jax.experimental import pallas as pl
from jax.experimental.pallas import tpu as pltpu
from jax.sharding import PartitionSpec as P

MESH = pl.DeviceIdType.MESH
VMEM_BYTES = 40 * 1024 * 1024
STEP_TILES = 8


def gelu_slope(pre_act):
    inner = 0.7978845608 * (pre_act + 0.044715 * pre_act * pre_act * pre_act)
    tanh_value = jnp.tanh(inner)
    return 0.5 * (1.0 + tanh_value) + 0.5 * pre_act * (
        1.0 - tanh_value * tanh_value
    ) * 0.7978845608 * (1.0 + 3.0 * 0.044715 * pre_act * pre_act)


def hop(index):
    return (index // 2 + 1) * (1 - 2 * (index % 2))


def vmem():
    return pl.BlockSpec(memory_space=pltpu.VMEM)


def smem():
    return pl.BlockSpec(memory_space=pltpu.SMEM)


def anywhere():
    return pl.BlockSpec(memory_space=pl.ANY)


def params(collective=None):
    if collective is None:
        return pltpu.CompilerParams(vmem_limit_bytes=VMEM_BYTES)
    return pltpu.CompilerParams(
        vmem_limit_bytes=VMEM_BYTES, collective_id=collective, has_side_effects=True
    )


def positions(num_blk, num_col):
    row, col = lax.axis_index("blk"), lax.axis_index("col")
    col_peer = [(row, lax.rem(col + step, num_col)) for step in range(1, num_col)]
    return row, col, col_peer


def greet(peers):
    barrier = pltpu.get_barrier_semaphore()
    for peer in peers:
        pl.semaphore_signal(barrier, inc=1, device_id=peer, device_id_type=MESH)
    pl.semaphore_wait(barrier, len(peers))


def push(src, dst, send_sem, recv_sem, peer):
    copy = pltpu.make_async_remote_copy(
        src_ref=src,
        dst_ref=dst,
        send_sem=send_sem,
        recv_sem=recv_sem,
        device_id=peer,
        device_id_type=MESH,
    )
    copy.start()
    return copy


def halo_peers(row, col, num_blk, num_hops, sign):
    return [
        (lax.rem(row + sign * hop(index) + num_blk, num_blk), col) for index in range(num_hops)
    ]


def pack_kernel(send_ref, feat_ref, out_ref):
    num_hops, _, width = out_ref.shape
    cap = send_ref.shape[2]
    side = width // cap
    for index in range(num_hops):
        for slot in range(cap):
            start = pl.multiple_of(send_ref[0, index, slot] * side, side)
            out_ref[index, :, slot * side : (slot + 1) * side] = feat_ref[:, pl.ds(start, side)]


def halo_kernel(
    num_blk, num_col, sbuf, feat_ref, cot_ref, recv_ref, feat_all, cot_all,
    halo_send, halo_recv, col_send, col_recv, own_sem,
):
    num_hops = sbuf.shape[0]
    part = feat_all.shape[2]
    row, col, col_peer = positions(num_blk, num_col)
    halo = halo_peers(row, col, num_blk, num_hops, 1)
    greet(halo + col_peer)
    copies = []
    for index in range(num_hops):
        copies.append(
            push(sbuf.at[index], recv_ref.at[index], halo_send.at[index], halo_recv.at[index], halo[index])
        )
    mine = pl.ds(pl.multiple_of(col * part, part), part)
    for at, (source, target) in enumerate(((feat_ref, feat_all), (cot_ref, cot_all))):
        for step, peer in enumerate(col_peer):
            theirs = pl.ds(pl.multiple_of(peer[1] * part, part), part)
            copies.append(
                push(
                    source.at[:, theirs], target.at[col], col_send.at[at, step],
                    col_recv.at[at, step], peer,
                )
            )
        own = pltpu.make_async_copy(source.at[:, mine], target.at[col], own_sem.at[at])
        own.start()
        copies.append(own)
    for copy in copies:
        copy.wait()


def aggregate_kernel(slots, dst_ref, src_ref, feat_ref, recv_ref, cnt_ref, agg_ref, floor_ref, acc):
    step = pl.program_id(0)
    blocks, rows, side = acc.shape
    dim = feat_ref.shape[0]
    num_hops = recv_ref.shape[0]
    cap = slots // num_hops
    tiles = cnt_ref.shape[0]

    @pl.when(step == 0)
    def _():
        acc[...] = jnp.zeros_like(acc)

    def add(tile, picked):
        counts = cnt_ref[tile].astype(jnp.float32).astype(jnp.bfloat16)
        left = jnp.concatenate([picked, jnp.ones((rows - dim, side), jnp.bfloat16)], axis=0)
        product = lax.dot_general(
            left, counts, (((1,), (1,)), ((), ())), preferred_element_type=jnp.float32
        )
        dst = dst_ref[step * tiles + tile]
        acc[dst] += product

    @pl.when(step * tiles < slots)
    def _():
        for tile in range(tiles):
            slot = src_ref[step * tiles + tile] - blocks
            start = pl.multiple_of(lax.rem(slot, cap) * side, side)
            add(tile, recv_ref[lax.div(slot, cap), :, pl.ds(start, side)])

    @pl.when(step * tiles >= slots)
    def _():
        for tile in range(tiles):
            start = pl.multiple_of(src_ref[step * tiles + tile] * side, side)
            add(tile, feat_ref[:, pl.ds(start, side)])

    @pl.when(step == pl.num_programs(0) - 1)
    def _():
        per_part = agg_ref.shape[2] // side
        for block in range(blocks):
            part, at = block // per_part, (block % per_part) * side
            floor = jnp.maximum(acc[block, dim : dim + 1, :], 1.0)
            floor_ref[part, :, at : at + side] = floor
            agg_ref[part, :, at : at + side] = (acc[block, :dim, :] / floor).astype(jnp.bfloat16)


def swap_kernel(num_blk, num_col, src_ref, dst_ref, send_sem, recv_sem, own_sem):
    row, col, col_peer = positions(num_blk, num_col)
    greet(col_peer)
    copies = [
        push(src_ref.at[peer[1]], dst_ref.at[col], send_sem.at[step], recv_sem.at[step], peer)
        for step, peer in enumerate(col_peer)
    ]
    own = pltpu.make_async_copy(src_ref.at[col], dst_ref.at[col], own_sem)
    own.start()
    for copy in copies:
        copy.wait()
    own.wait()


def dense_kernel(
    chunk, feat_ref, agg_ref, cot_ref, floor_ref, ws_ref, wn_ref, bias_ref,
    scaled_ref, self_ref, grad_ref, acc,
):
    width, nodes = feat_ref.shape
    parts, dim, _ = scaled_ref.shape
    col = lax.axis_index("col")
    self_weight, neigh_weight = ws_ref[...], wn_ref[...]
    first = (((0,), (0,)), ((), ()))
    last = (((1,), (1,)), ((), ()))
    bias = bias_ref[...]
    for start in range(0, nodes, chunk):
        at = slice(start, start + chunk)
        feat, agg = feat_ref[:, at], agg_ref[:, at]
        pre_act = (
            lax.dot_general(self_weight, feat, first, preferred_element_type=jnp.float32)
            + lax.dot_general(neigh_weight, agg, first, preferred_element_type=jnp.float32)
            + bias
        )
        dz = (cot_ref[:, at].astype(jnp.float32) * gelu_slope(pre_act)).astype(jnp.bfloat16)
        floor = floor_ref[col, :, at]
        neigh = jnp.dot(neigh_weight, dz, preferred_element_type=jnp.float32) / floor
        own = jnp.dot(self_weight, dz, preferred_element_type=jnp.float32)
        for part in range(parts):
            rows = slice(part * dim, (part + 1) * dim)
            scaled_ref[part, :, at] = neigh[rows].astype(jnp.bfloat16)
            self_ref[part, :, at] = own[rows].astype(jnp.bfloat16)
        ones = jnp.ones((16, chunk), jnp.bfloat16)
        left = jnp.concatenate([feat, agg, ones], axis=0)
        grads = lax.dot_general(left, dz, last, preferred_element_type=jnp.float32)
        if start == 0:
            acc[...] = grads
        else:
            acc[...] += grads
    for part in range(parts):
        rows = slice(part * dim, (part + 1) * dim)
        grad_ref[part, :dim, :width] = acc[rows, :].astype(jnp.bfloat16)
        grad_ref[part, dim:, :width] = acc[width + part * dim : width + (part + 1) * dim, :].astype(
            jnp.bfloat16
        )
        bias_row = acc[2 * width : 2 * width + 1, rows].astype(jnp.bfloat16)
        grad_ref[part, :, width : width + dim] = jnp.broadcast_to(bias_row, (2 * dim, dim))
        if dim < grad_ref.shape[2] - width:
            rest = grad_ref.shape[2] - width - dim
            grad_ref[part, :, width + dim :] = jnp.zeros((2 * dim, rest), jnp.bfloat16)


def spread_kernel(slots, dst_ref, src_ref, scaled_ref, cnt_ref, ret_ref, back_ref):
    step = pl.program_id(0)
    num_hops, _, width = ret_ref.shape
    cap = slots // num_hops
    side = width // cap
    blocks = back_ref.shape[0]
    per_part = scaled_ref.shape[2] // side
    tiles = cnt_ref.shape[0]

    @pl.when(step == 0)
    def _():
        back_ref[...] = jnp.zeros_like(back_ref)

    def contribution(tile):
        dst = dst_ref[step * tiles + tile]
        start = pl.multiple_of(lax.rem(dst, per_part) * side, side)
        picked = scaled_ref[lax.div(dst, per_part), :, pl.ds(start, side)]
        counts = cnt_ref[tile].astype(jnp.float32).astype(jnp.bfloat16)
        return jnp.dot(picked, counts, preferred_element_type=jnp.float32)

    @pl.when(step * tiles < slots)
    def _():
        for tile in range(tiles):
            slot = src_ref[step * tiles + tile] - blocks
            start = pl.multiple_of(lax.rem(slot, cap) * side, side)
            ret_ref[lax.div(slot, cap), :, pl.ds(start, side)] = contribution(tile).astype(
                jnp.bfloat16
            )

    @pl.when(step * tiles >= slots)
    def _():
        for tile in range(tiles):
            back_ref[src_ref[step * tiles + tile]] += contribution(tile)


def return_kernel(
    num_blk, num_col, ret_ref, self_ref, grad_ref, came_ref, self_all, grad_out, bias_out,
    col_buf, rs_src, rs_buf, piece,
    halo_send, halo_recv, col_send, col_recv, rs_send, rs_recv, ag_send, ag_recv, own_sem,
):
    num_hops = ret_ref.shape[0]
    row, col, col_peer = positions(num_blk, num_col)
    width = piece.shape[1]
    halo = halo_peers(row, col, num_blk, num_hops, -1)
    ring = [(lax.rem(row + step, num_blk), col) for step in range(1, num_blk)]
    greet(ring + col_peer)
    first = [
        push(grad_ref.at[peer[1]], col_buf.at[step], col_send.at[0, step], col_recv.at[0, step], peer)
        for step, peer in enumerate(col_peer)
    ]
    later = [
        push(ret_ref.at[index], came_ref.at[index], halo_send.at[index], halo_recv.at[index], halo[index])
        for index in range(num_hops)
    ]
    later += [
        push(self_ref.at[peer[1]], self_all.at[col], col_send.at[1, step], col_recv.at[1, step], peer)
        for step, peer in enumerate(col_peer)
    ]
    own = pltpu.make_async_copy(self_ref.at[col], self_all.at[col], own_sem)
    own.start()
    for copy in first:
        copy.wait()
    for index in range(num_blk):
        total = grad_ref[col, index].astype(jnp.float32)
        for step in range(num_col - 1):
            total += col_buf[step, index].astype(jnp.float32)
        rs_src[index] = total.astype(jnp.bfloat16)
    scatter = [
        push(rs_src.at[peer[0]], rs_buf.at[step], rs_send.at[step], rs_recv.at[step], peer)
        for step, peer in enumerate(ring)
    ]
    total = rs_src[row].astype(jnp.float32)
    for step, copy in enumerate(scatter):
        copy.wait()
        total += rs_buf[step].astype(jnp.float32)
    bias_out[...] = total[0:1, width:]
    piece[...] = total[:, :width].astype(jnp.bfloat16)
    grad_out[row] = piece[...]
    gather = [
        push(piece, grad_out.at[row], ag_send.at[step], ag_recv.at[step], peer)
        for step, peer in enumerate(ring)
    ]
    for copy in gather + later:
        copy.wait()
    own.wait()


def finish_kernel(send_ref, self_ref, back_ref, came_ref, out_ref, acc):
    blocks, _, side = acc.shape
    num_hops, _, width = came_ref.shape
    cap = width // side
    acc[...] = back_ref[...]
    for index in range(num_hops):
        for slot in range(cap):
            came = came_ref[index, :, slot * side : (slot + 1) * side]
            acc[send_ref[0, index, slot]] += came.astype(jnp.float32)
    per_part = self_ref.shape[2] // side
    for block in range(blocks):
        at = (block % per_part) * side
        own = self_ref[block // per_part, :, at : at + side].astype(jnp.float32)
        out_ref[:, block * side : (block + 1) * side] = (acc[block] + own).astype(jnp.bfloat16)


def per_device(
    num_blk, num_col,
    node_feats, tile_dst, tile_src, tile_cnt, send_blk, self_weight, neigh_weight, bias, cotangent,
):
    half, full = jnp.bfloat16, jnp.float32
    dim, rows = node_feats.shape
    tiles, side, _ = tile_cnt.shape
    blocks = rows // side
    num_hops, cap = send_blk.shape[1:]
    slots = num_hops * cap
    part = rows // num_col
    width = self_weight.shape[0]
    dma = pltpu.SemaphoreType.DMA
    shape = jax.ShapeDtypeStruct
    peers = max(num_col - 1, 1)
    split = shape((num_col, dim, part), half)
    slot_shape = shape((num_hops, dim, cap * side), half)

    outgoing = pl.pallas_call(
        pack_kernel,
        out_shape=slot_shape,
        in_specs=[smem(), vmem()],
        out_specs=vmem(),
        compiler_params=params(),
        name="pack",
    )(send_blk, node_feats)
    received, feat_all, cot_all = pl.pallas_call(
        functools.partial(halo_kernel, num_blk, num_col),
        out_shape=(slot_shape, split, split),
        in_specs=[anywhere()] * 3,
        out_specs=(anywhere(),) * 3,
        scratch_shapes=[
            dma((num_hops,)), dma((num_hops,)), dma((2, peers)), dma((2, peers)), dma((2,)),
        ],
        compiler_params=params(0),
        name="halo",
    )(outgoing, node_feats, cotangent)

    steps = tiles // STEP_TILES
    cnt_spec = pl.BlockSpec((STEP_TILES, side, side), lambda step: (step, 0, 0))
    whole = lambda dims: pl.BlockSpec(dims, lambda step: (0,) * len(dims))
    aggregate, floor = pl.pallas_call(
        functools.partial(aggregate_kernel, slots),
        grid=(steps,),
        out_shape=(split, shape((num_col, 1, part), full)),
        in_specs=[smem(), smem(), whole((dim, rows)), whole(slot_shape.shape), cnt_spec],
        out_specs=(whole(split.shape), whole((num_col, 1, part))),
        scratch_shapes=[pltpu.VMEM((blocks, dim + 16, side), full)],
        compiler_params=params(),
        name="aggregate",
    )(tile_dst, tile_src, node_feats, received, tile_cnt)

    def swap(array, collective, name):
        return pl.pallas_call(
            functools.partial(swap_kernel, num_blk, num_col),
            out_shape=split,
            in_specs=[anywhere()],
            out_specs=anywhere(),
            scratch_shapes=[dma((peers,)), dma((peers,)), dma(())],
            compiler_params=params(collective),
            name=name,
        )(array)

    agg_all = swap(aggregate, 1, "swap_aggregate")
    lanes = width + 128
    scaled, own_part, grads = pl.pallas_call(
        functools.partial(dense_kernel, min(part, 256)),
        out_shape=(split, split, shape((num_col, 2 * dim, lanes), half)),
        in_specs=[vmem()] * 7,
        out_specs=(vmem(),) * 3,
        scratch_shapes=[pltpu.VMEM((2 * width + 16, width), full)],
        compiler_params=params(),
        name="dense",
    )(
        feat_all.reshape(width, part), agg_all.reshape(width, part), cot_all.reshape(width, part),
        floor, self_weight, neigh_weight, bias.reshape(width, 1),
    )
    scaled_all = swap(scaled, 2, "swap_scaled")
    returning, back_local = pl.pallas_call(
        functools.partial(spread_kernel, slots),
        grid=(steps,),
        out_shape=(slot_shape, shape((blocks, dim, side), full)),
        in_specs=[smem(), smem(), whole(split.shape), cnt_spec],
        out_specs=(whole(slot_shape.shape), whole((blocks, dim, side))),
        compiler_params=params(),
        name="spread",
    )(tile_dst, tile_src, scaled_all, tile_cnt)

    span = 2 * dim // num_blk
    ring = num_blk - 1
    came, own_all, grad_sum, bias_sum = pl.pallas_call(
        functools.partial(return_kernel, num_blk, num_col),
        out_shape=(slot_shape, split, shape((num_blk, span, width), half), shape((1, 128), full)),
        in_specs=[anywhere(), anywhere(), vmem()],
        out_specs=(anywhere(), anywhere(), vmem(), vmem()),
        scratch_shapes=[
            pltpu.VMEM((peers, num_blk, span, lanes), half),
            pltpu.VMEM((num_blk, span, lanes), half),
            pltpu.VMEM((ring, span, lanes), half),
            pltpu.VMEM((span, width), half),
            dma((num_hops,)), dma((num_hops,)), dma((2, peers)), dma((2, peers)),
            dma((ring,)), dma((ring,)), dma((ring,)), dma((ring,)), dma(()),
        ],
        compiler_params=params(3),
        name="give_back",
    )(returning, own_part, grads.reshape(num_col, num_blk, span, lanes))

    grad_feats = pl.pallas_call(
        finish_kernel,
        out_shape=shape((dim, rows), half),
        in_specs=[smem(), vmem(), vmem(), vmem()],
        out_specs=vmem(),
        scratch_shapes=[pltpu.VMEM((blocks, dim, side), full)],
        compiler_params=params(),
        name="finish",
    )(send_blk, own_all, back_local, came)
    grad_both = grad_sum.reshape(2 * dim, width).astype(full)
    return (grad_feats, grad_both[:dim], grad_both[dim:], bias_sum[0, :dim])


def solution(mesh):
    placed = (
        P("col", "blk"),
        P("blk"),
        P("blk"),
        P("blk", None, None),
        P("blk", None, None),
        P(),
        P(),
        P(),
        P("col", "blk"),
    )
    return jax.shard_map(
        functools.partial(per_device, mesh.shape["blk"], mesh.shape["col"]),
        mesh=mesh,
        in_specs=placed,
        out_specs=(P("col", "blk"), P("col", None), P("col", None), P("col")),
        check_vma=False,
    )
```

```python
import functools

import jax
import jax.numpy as jnp
from jax import lax
from jax.experimental import pallas as pl
from jax.experimental.pallas import tpu as pltpu
from jax.sharding import PartitionSpec as P

MESH = pl.DeviceIdType.MESH
VMEM_BYTES = 40 * 1024 * 1024
STEP_TILES = 8


def gelu_slope(pre_act):
    inner = 0.7978845608 * (pre_act + 0.044715 * pre_act * pre_act * pre_act)
    tanh_value = jnp.tanh(inner)
    return 0.5 * (1.0 + tanh_value) + 0.5 * pre_act * (
        1.0 - tanh_value * tanh_value
    ) * 0.7978845608 * (1.0 + 3.0 * 0.044715 * pre_act * pre_act)


def hop(index):
    return (index // 2 + 1) * (1 - 2 * (index % 2))


def vmem():
    return pl.BlockSpec(memory_space=pltpu.VMEM)


def smem():
    return pl.BlockSpec(memory_space=pltpu.SMEM)


def anywhere():
    return pl.BlockSpec(memory_space=pl.ANY)


def params(collective=None):
    if collective is None:
        return pltpu.CompilerParams(vmem_limit_bytes=VMEM_BYTES)
    return pltpu.CompilerParams(
        vmem_limit_bytes=VMEM_BYTES, collective_id=collective, has_side_effects=True
    )


def positions(num_blk, num_col):
    row, col = lax.axis_index("blk"), lax.axis_index("col")
    col_peer = [(row, lax.rem(col + step, num_col)) for step in range(1, num_col)]
    return row, col, col_peer


def greet(peers):
    barrier = pltpu.get_barrier_semaphore()
    for peer in peers:
        pl.semaphore_signal(barrier, inc=1, device_id=peer, device_id_type=MESH)
    pl.semaphore_wait(barrier, len(peers))


def push(src, dst, send_sem, recv_sem, peer):
    copy = pltpu.make_async_remote_copy(
        src_ref=src,
        dst_ref=dst,
        send_sem=send_sem,
        recv_sem=recv_sem,
        device_id=peer,
        device_id_type=MESH,
    )
    copy.start()
    return copy


def halo_peers(row, col, num_blk, num_hops, sign):
    return [
        (lax.rem(row + sign * hop(index) + num_blk, num_blk), col) for index in range(num_hops)
    ]


def pack_kernel(send_ref, feat_ref, out_ref):
    num_hops, _, width = out_ref.shape
    cap = send_ref.shape[2]
    side = width // cap
    for index in range(num_hops):
        for slot in range(cap):
            start = pl.multiple_of(send_ref[0, index, slot] * side, side)
            out_ref[index, :, slot * side : (slot + 1) * side] = feat_ref[:, pl.ds(start, side)]


def halo_kernel(
    num_blk, num_col, sbuf, feat_ref, cot_ref, recv_ref, feat_all, cot_all,
    halo_send, halo_recv, col_send, col_recv, own_sem,
):
    num_hops = sbuf.shape[0]
    part = feat_all.shape[2]
    row, col, col_peer = positions(num_blk, num_col)
    halo = halo_peers(row, col, num_blk, num_hops, 1)
    greet(halo + col_peer)
    copies = []
    for index in range(num_hops):
        copies.append(
            push(sbuf.at[index], recv_ref.at[index], halo_send.at[index], halo_recv.at[index], halo[index])
        )
    mine = pl.ds(pl.multiple_of(col * part, part), part)
    for at, (source, target) in enumerate(((feat_ref, feat_all), (cot_ref, cot_all))):
        for step, peer in enumerate(col_peer):
            theirs = pl.ds(pl.multiple_of(peer[1] * part, part), part)
            copies.append(
                push(
                    source.at[:, theirs], target.at[col], col_send.at[at, step],
                    col_recv.at[at, step], peer,
                )
            )
        own = pltpu.make_async_copy(source.at[:, mine], target.at[col], own_sem.at[at])
        own.start()
        copies.append(own)
    for copy in copies:
        copy.wait()


def aggregate_kernel(slots, dst_ref, src_ref, feat_ref, recv_ref, cnt_ref, agg_ref, floor_ref,
                     half_ref, slot_dst_ref, acc):
    step = pl.program_id(0)
    blocks, rows, side = acc.shape
    dim = feat_ref.shape[0]
    num_hops = recv_ref.shape[0]
    cap = slots // num_hops
    tiles = cnt_ref.shape[0]

    @pl.when(step == 0)
    def _():
        acc[...] = jnp.zeros_like(acc)

    def add(tile, picked, place):
        counts = cnt_ref[tile].astype(jnp.float32).astype(jnp.bfloat16)
        half_ref[place] = counts
        left = jnp.concatenate([picked, jnp.ones((rows - dim, side), jnp.bfloat16)], axis=0)
        product = lax.dot_general(
            left, counts, (((1,), (1,)), ((), ())), preferred_element_type=jnp.float32
        )
        dst = dst_ref[step * tiles + tile]
        acc[dst] += product

    @pl.when(step * tiles < slots)
    def _():
        for tile in range(tiles):
            slot = src_ref[step * tiles + tile] - blocks
            start = pl.multiple_of(lax.rem(slot, cap) * side, side)
            add(tile, recv_ref[lax.div(slot, cap), :, pl.ds(start, side)], slot)
            slot_dst_ref[slot] = dst_ref[step * tiles + tile]

    @pl.when(step * tiles >= slots)
    def _():
        for tile in range(tiles):
            start = pl.multiple_of(src_ref[step * tiles + tile] * side, side)
            add(tile, feat_ref[:, pl.ds(start, side)], step * tiles + tile)

    @pl.when(step == pl.num_programs(0) - 1)
    def _():
        per_part = agg_ref.shape[2] // side
        for block in range(blocks):
            part, at = block // per_part, (block % per_part) * side
            floor = jnp.maximum(acc[block, dim : dim + 1, :], 1.0)
            floor_ref[part, :, at : at + side] = floor
            agg_ref[part, :, at : at + side] = (acc[block, :dim, :] / floor).astype(jnp.bfloat16)


def swap_kernel(num_blk, num_col, src_ref, dst_ref, send_sem, recv_sem, own_sem):
    row, col, col_peer = positions(num_blk, num_col)
    greet(col_peer)
    copies = [
        push(src_ref.at[peer[1]], dst_ref.at[col], send_sem.at[step], recv_sem.at[step], peer)
        for step, peer in enumerate(col_peer)
    ]
    own = pltpu.make_async_copy(src_ref.at[col], dst_ref.at[col], own_sem)
    own.start()
    for copy in copies:
        copy.wait()
    own.wait()


def dense_kernel(
    chunk, feat_ref, agg_ref, cot_ref, floor_ref, ws_ref, wn_ref, bias_ref,
    *outs,
):
    scaled_refs, (self_ref, grad_ref, acc) = outs[:-3], outs[-3:]
    width, nodes = feat_ref.shape
    parts, _, piece, side = scaled_refs[0].shape
    dim = self_ref.shape[1]
    col = lax.axis_index("col")
    self_weight, neigh_weight = ws_ref[...], wn_ref[...]
    first = (((0,), (0,)), ((), ()))
    last = (((1,), (1,)), ((), ()))
    bias = bias_ref[...]
    for start in range(0, nodes, chunk):
        at = slice(start, start + chunk)
        feat, agg = feat_ref[:, at], agg_ref[:, at]
        pre_act = (
            lax.dot_general(self_weight, feat, first, preferred_element_type=jnp.float32)
            + lax.dot_general(neigh_weight, agg, first, preferred_element_type=jnp.float32)
            + bias
        )
        dz = (cot_ref[:, at].astype(jnp.float32) * gelu_slope(pre_act)).astype(jnp.bfloat16)
        floor = floor_ref[col, :, at]
        neigh = jnp.dot(neigh_weight, dz, preferred_element_type=jnp.float32) / floor
        own = jnp.dot(self_weight, dz, preferred_element_type=jnp.float32)
        for part in range(parts):
            rows = slice(part * dim, (part + 1) * dim)
            for index, scaled_ref in enumerate(scaled_refs):
                top = part * dim + index * piece
                for left in range(0, chunk, side):
                    scaled_ref[part, (start + left) // side] = neigh[
                        top : top + piece, left : left + side
                    ].astype(jnp.bfloat16)
            self_ref[part, :, at] = own[rows].astype(jnp.bfloat16)
        ones = jnp.ones((16, chunk), jnp.bfloat16)
        left = jnp.concatenate([feat, agg, ones], axis=0)
        grads = lax.dot_general(left, dz, last, preferred_element_type=jnp.float32)
        if start == 0:
            acc[...] = grads
        else:
            acc[...] += grads
    for part in range(parts):
        rows = slice(part * dim, (part + 1) * dim)
        grad_ref[part, :dim, :width] = acc[rows, :].astype(jnp.bfloat16)
        grad_ref[part, dim:, :width] = acc[width + part * dim : width + (part + 1) * dim, :].astype(
            jnp.bfloat16
        )
        bias_row = acc[2 * width : 2 * width + 1, rows].astype(jnp.bfloat16)
        grad_ref[part, :, width : width + dim] = jnp.broadcast_to(bias_row, (2 * dim, dim))
        if dim < grad_ref.shape[2] - width:
            rest = grad_ref.shape[2] - width - dim
            grad_ref[part, :, width + dim :] = jnp.zeros((2 * dim, rest), jnp.bfloat16)


def return_kernel(
    num_blk, num_col, slot_dst, half_ref, scaled_a, scaled_b, self_ref, grad_ref,
    all_a, all_b, came_ref, self_all, grad_out, bias_out,
    ret, col_buf, core_src, core_buf, mid_src, mid_buf, far_src, far_buf,
    halo_send, halo_recv, col_send, col_recv, up_send, up_recv, down_send, down_recv, own_sem,
):
    slots = ret.shape[1]
    num_hops = halo_send.shape[1]
    cap = slots // num_hops
    blocks = scaled_a.shape[1]
    row, col, col_peer = positions(num_blk, num_col)
    far_size = num_blk // 4
    core, mid, far = row % 2, (row // 2) % 2, row // 4
    width = grad_out.shape[4]
    halo = halo_peers(row, col, num_blk, num_hops, -1)
    core_peer = (far * 4 + mid * 2 + 1 - core, col)
    mid_peer = (far * 4 + (1 - mid) * 2 + core, col)
    far_peers = [((far + step) % far_size * 4 + mid * 2 + core, col) for step in range(1, far_size)]
    greet(halo + [core_peer, mid_peer] + far_peers + col_peer)

    def across(at, source, target):
        return [
            push(source.at[peer[1]], target(step), col_send.at[at, step], col_recv.at[at, step], peer)
            for step, peer in enumerate(col_peer)
        ]

    def settle(copies):
        for copy in copies:
            copy.wait()

    mine = pl.ds(col * blocks, blocks)
    owns = []
    for at, (source, target) in enumerate(
        ((scaled_a.at[col], all_a.at[mine]), (scaled_b.at[col], all_b.at[mine]), (self_ref.at[col], self_all.at[col]))
    ):
        own = pltpu.make_async_copy(source, target, own_sem.at[at])
        own.start()
        owns.append(own)
    grads = across(0, grad_ref, lambda step: col_buf.at[step])
    ins = [across(1, scaled_a, lambda step: all_a.at[mine]), across(2, scaled_b, lambda step: all_b.at[mine])]

    def spread(index, source):
        def body(slot, carry):
            picked = source[slot_dst[slot]]
            ret[index, slot] = jnp.dot(
                picked, half_ref[slot], preferred_element_type=jnp.float32
            ).astype(jnp.bfloat16)
            return carry

        lax.fori_loop(0, slots, body, 0, unroll=8)

    def give(index):
        copies = []
        for at in range(num_hops):
            part = pl.ds(at * cap, cap)
            copies.append(
                push(
                    ret.at[index, part], came_ref.at[index, part], halo_send.at[index, at],
                    halo_recv.at[index, at], halo[at],
                )
            )
        return copies

    settle(grads)
    total = grad_ref[col].astype(jnp.float32)
    for step in range(num_col - 1):
        total += col_buf[step].astype(jnp.float32)
    core_src[...] = total.astype(jnp.bfloat16)
    up = push(core_src.at[1 - core], core_buf, up_send.at[0], up_recv.at[0], core_peer)
    settle(ins[0])
    owns[0].wait()
    spread(0, all_a)
    up.wait()
    mid_src[...] = (core_src[core].astype(jnp.float32) + core_buf[...].astype(jnp.float32)).astype(jnp.bfloat16)
    up = push(mid_src.at[1 - mid], mid_buf, up_send.at[1], up_recv.at[1], mid_peer)
    later = give(0)
    later += across(3, self_ref, lambda step: self_all.at[col])
    up.wait()
    far_src[...] = (mid_src[mid].astype(jnp.float32) + mid_buf[...].astype(jnp.float32)).astype(jnp.bfloat16)
    ups = [
        push(far_src.at[peer[0] // 4], far_buf.at[step], up_send.at[2 + step], up_recv.at[2 + step], peer)
        for step, peer in enumerate(far_peers)
    ]
    settle(ins[1])
    owns[1].wait()
    spread(1, all_b)
    later += give(1)
    settle(ups)
    total = far_src[far].astype(jnp.float32)
    for step in range(far_size - 1):
        total += far_buf[step].astype(jnp.float32)
    bias_out[...] = total[0:1, width:]
    grad_out[core, mid, far] = total[:, :width].astype(jnp.bfloat16)
    settle([
        push(
            grad_out.at[core, mid, far], grad_out.at[core, mid, far], down_send.at[2 + step],
            down_recv.at[2 + step], peer,
        )
        for step, peer in enumerate(far_peers)
    ])
    settle([push(grad_out.at[core, mid], grad_out.at[core, mid], down_send.at[1], down_recv.at[1], mid_peer)])
    settle([push(grad_out.at[core], grad_out.at[core], down_send.at[0], down_recv.at[0], core_peer)])
    settle(later)
    owns[2].wait()


def finish_kernel(
    slots, send_ref, dst_ref, src_ref, half_ref, all_a, all_b, self_ref, came_ref, out_ref, acc
):
    blocks, _, side = acc.shape
    num_hops, cap = send_ref.shape[1:]
    piece = all_a.shape[1]
    acc[...] = jnp.zeros_like(acc)
    for tile in range(slots, dst_ref.shape[0]):
        dst = dst_ref[tile]
        picked = jnp.concatenate([all_a[dst], all_b[dst]], axis=0)
        acc[src_ref[tile]] += jnp.dot(picked, half_ref[tile], preferred_element_type=jnp.float32)
    for slot in range(slots):
        came = jnp.concatenate([came_ref[0, slot], came_ref[1, slot]], axis=0)
        acc[send_ref[0, slot // cap, slot % cap]] += came.astype(jnp.float32)
    per_part = self_ref.shape[2] // side
    for block in range(blocks):
        at = (block % per_part) * side
        own = self_ref[block // per_part, :, at : at + side].astype(jnp.float32)
        out_ref[:, block * side : (block + 1) * side] = (acc[block] + own).astype(jnp.bfloat16)


def per_device(
    num_blk, num_col,
    node_feats, tile_dst, tile_src, tile_cnt, send_blk, self_weight, neigh_weight, bias, cotangent,
):
    half, full = jnp.bfloat16, jnp.float32
    dim, rows = node_feats.shape
    tiles, side, _ = tile_cnt.shape
    blocks = rows // side
    num_hops, cap = send_blk.shape[1:]
    slots = num_hops * cap
    part = rows // num_col
    width = self_weight.shape[0]
    dma = pltpu.SemaphoreType.DMA
    shape = jax.ShapeDtypeStruct
    peers = max(num_col - 1, 1)
    split = shape((num_col, dim, part), half)
    slot_shape = shape((num_hops, dim, cap * side), half)

    outgoing = pl.pallas_call(
        pack_kernel,
        out_shape=slot_shape,
        in_specs=[smem(), vmem()],
        out_specs=vmem(),
        compiler_params=params(),
        name="pack",
    )(send_blk, node_feats)
    received, feat_all, cot_all = pl.pallas_call(
        functools.partial(halo_kernel, num_blk, num_col),
        out_shape=(slot_shape, split, split),
        in_specs=[anywhere()] * 3,
        out_specs=(anywhere(),) * 3,
        scratch_shapes=[
            dma((num_hops,)), dma((num_hops,)), dma((2, peers)), dma((2, peers)), dma((2,)),
        ],
        compiler_params=params(0),
        name="halo",
    )(outgoing, node_feats, cotangent)

    steps = tiles // STEP_TILES
    cnt_spec = pl.BlockSpec((STEP_TILES, side, side), lambda step: (step, 0, 0))
    whole = lambda dims: pl.BlockSpec(dims, lambda step: (0,) * len(dims))
    aggregate, floor, half_cnt, slot_dst = pl.pallas_call(
        functools.partial(aggregate_kernel, slots),
        grid=(steps,),
        out_shape=(
            split, shape((num_col, 1, part), full), shape((tiles, side, side), half),
            shape((slots,), jnp.int32),
        ),
        in_specs=[smem(), smem(), whole((dim, rows)), whole(slot_shape.shape), cnt_spec],
        out_specs=(whole(split.shape), whole((num_col, 1, part)), whole((tiles, side, side)), smem()),
        scratch_shapes=[pltpu.VMEM((blocks, dim + 16, side), full)],
        compiler_params=params(),
        name="aggregate",
    )(tile_dst, tile_src, node_feats, received, tile_cnt)

    def swap(array, collective, name):
        return pl.pallas_call(
            functools.partial(swap_kernel, num_blk, num_col),
            out_shape=split,
            in_specs=[anywhere()],
            out_specs=anywhere(),
            scratch_shapes=[dma((peers,)), dma((peers,)), dma(())],
            compiler_params=params(collective),
            name=name,
        )(array)

    agg_all = swap(aggregate, 1, "swap_aggregate")
    lanes = width + 128
    per_part = part // side
    piece = dim // 2
    scaled_shape = shape((num_col, per_part, piece, side), half)
    scaled_a, scaled_b, own_part, grads = pl.pallas_call(
        functools.partial(dense_kernel, min(part, 256)),
        out_shape=(scaled_shape, scaled_shape, split, shape((num_col, 2 * dim, lanes), half)),
        in_specs=[vmem()] * 7,
        out_specs=(vmem(),) * 4,
        scratch_shapes=[pltpu.VMEM((2 * width + 16, width), full)],
        compiler_params=params(),
        name="dense",
    )(
        feat_all.reshape(width, part), agg_all.reshape(width, part), cot_all.reshape(width, part),
        floor, self_weight, neigh_weight, bias.reshape(width, 1),
    )

    far_size = num_blk // 4
    span = 2 * dim // num_blk
    all_shape = shape((blocks, piece, side), half)
    level = lambda *lead: pltpu.VMEM(lead + (span, lanes), half)
    all_a, all_b, came, own_all, grad_sum, bias_sum = pl.pallas_call(
        functools.partial(return_kernel, num_blk, num_col),
        out_shape=(
            all_shape, all_shape, shape((2, slots, piece, side), half), split,
            shape((2, 2, far_size, span, width), half), shape((1, 128), full),
        ),
        in_specs=[smem()] + [vmem()] * 5,
        out_specs=(vmem(),) * 6,
        scratch_shapes=[
            pltpu.VMEM((2, slots, piece, side), half),
            level(peers, 2, 2, far_size), level(2, 2, far_size), level(2, far_size),
            level(2, far_size), level(far_size), level(far_size), level(max(far_size - 1, 1)),
            dma((2, num_hops)), dma((2, num_hops)), dma((4, peers)), dma((4, peers)),
            dma((far_size + 1,)), dma((far_size + 1,)), dma((far_size + 1,)), dma((far_size + 1,)),
            dma((3,)),
        ],
        compiler_params=params(2),
        name="give_back",
    )(
        slot_dst, half_cnt, scaled_a, scaled_b, own_part,
        grads.reshape(num_col, 2, 2, far_size, span, lanes),
    )

    grad_feats = pl.pallas_call(
        functools.partial(finish_kernel, slots),
        out_shape=shape((dim, rows), half),
        in_specs=[smem()] * 3 + [vmem()] * 5,
        out_specs=vmem(),
        scratch_shapes=[pltpu.VMEM((blocks, dim, side), full)],
        compiler_params=params(),
        name="finish",
    )(send_blk, tile_dst, tile_src, half_cnt, all_a, all_b, own_all, came)
    grad_both = grad_sum.reshape(2 * dim, width).astype(full)
    return (grad_feats, grad_both[:dim], grad_both[dim:], bias_sum[0, :dim])


def solution(mesh):
    placed = (
        P("col", "blk"),
        P("blk"),
        P("blk"),
        P("blk", None, None),
        P("blk", None, None),
        P(),
        P(),
        P(),
        P("col", "blk"),
    )
    return jax.shard_map(
        functools.partial(per_device, mesh.shape["blk"], mesh.shape["col"]),
        mesh=mesh,
        in_specs=placed,
        out_specs=(P("col", "blk"), P("col", None), P("col", None), P("col")),
        check_vma=False,
    )
```

```python
import functools

import jax
import jax.numpy as jnp
from jax import lax
from jax.experimental import pallas as pl
from jax.experimental.pallas import tpu as pltpu
from jax.sharding import PartitionSpec as P

MESH = pl.DeviceIdType.MESH
VMEM_BYTES = 40 * 1024 * 1024
STEP_TILES = 8


def gelu_slope(pre_act):
    inner = 0.7978845608 * (pre_act + 0.044715 * pre_act * pre_act * pre_act)
    tanh_value = jnp.tanh(inner)
    return 0.5 * (1.0 + tanh_value) + 0.5 * pre_act * (
        1.0 - tanh_value * tanh_value
    ) * 0.7978845608 * (1.0 + 3.0 * 0.044715 * pre_act * pre_act)


def hop(index):
    return (index // 2 + 1) * (1 - 2 * (index % 2))


def vmem():
    return pl.BlockSpec(memory_space=pltpu.VMEM)


def smem():
    return pl.BlockSpec(memory_space=pltpu.SMEM)


def anywhere():
    return pl.BlockSpec(memory_space=pl.ANY)


def params(collective=None):
    if collective is None:
        return pltpu.CompilerParams(vmem_limit_bytes=VMEM_BYTES)
    return pltpu.CompilerParams(
        vmem_limit_bytes=VMEM_BYTES, collective_id=collective, has_side_effects=True
    )


def added(one, other):
    return one.astype(jnp.float32) + other.astype(jnp.float32)


def positions(num_blk, num_col):
    row, col = lax.axis_index("blk"), lax.axis_index("col")
    col_peer = [(row, lax.rem(col + step, num_col)) for step in range(1, num_col)]
    return row, col, col_peer


def greet(peers):
    barrier = pltpu.get_barrier_semaphore()
    for peer in peers:
        pl.semaphore_signal(barrier, inc=1, device_id=peer, device_id_type=MESH)
    pl.semaphore_wait(barrier, len(peers))


def push(src, dst, send_sem, recv_sem, peer):
    copy = pltpu.make_async_remote_copy(
        src_ref=src,
        dst_ref=dst,
        send_sem=send_sem,
        recv_sem=recv_sem,
        device_id=peer,
        device_id_type=MESH,
    )
    copy.start()
    return copy


def halo_peers(row, col, num_blk, num_hops, sign):
    return [
        (lax.rem(row + sign * hop(index) + num_blk, num_blk), col) for index in range(num_hops)
    ]


def pack_kernel(send_ref, feat_ref, out_ref):
    num_hops, _, width = out_ref.shape
    cap = send_ref.shape[2]
    side = width // cap
    for index in range(num_hops):
        for slot in range(cap):
            start = pl.multiple_of(send_ref[0, index, slot] * side, side)
            out_ref[index, :, slot * side : (slot + 1) * side] = feat_ref[:, pl.ds(start, side)]


def halo_kernel(
    num_blk, num_col, sbuf, feat_ref, cot_ref, recv_ref, feat_all, cot_all,
    halo_send, halo_recv, col_send, col_recv, own_sem,
):
    num_hops = sbuf.shape[0]
    part = feat_all.shape[2]
    row, col, col_peer = positions(num_blk, num_col)
    halo = halo_peers(row, col, num_blk, num_hops, 1)
    greet(halo + col_peer)
    copies = []
    for index in range(num_hops):
        copies.append(
            push(sbuf.at[index], recv_ref.at[index], halo_send.at[index], halo_recv.at[index], halo[index])
        )
    mine = pl.ds(pl.multiple_of(col * part, part), part)
    for at, (source, target) in enumerate(((feat_ref, feat_all), (cot_ref, cot_all))):
        for step, peer in enumerate(col_peer):
            theirs = pl.ds(pl.multiple_of(peer[1] * part, part), part)
            copies.append(
                push(
                    source.at[:, theirs], target.at[col], col_send.at[at, step],
                    col_recv.at[at, step], peer,
                )
            )
        own = pltpu.make_async_copy(source.at[:, mine], target.at[col], own_sem.at[at])
        own.start()
        copies.append(own)
    for copy in copies:
        copy.wait()


def aggregate_kernel(slots, dst_ref, src_ref, feat_ref, recv_ref, cnt_ref, agg_ref, floor_ref,
                     half_ref, slot_dst_ref, acc):
    step = pl.program_id(0)
    blocks, rows, side = acc.shape
    dim = feat_ref.shape[0]
    num_hops = recv_ref.shape[0]
    cap = slots // num_hops
    tiles = cnt_ref.shape[0]

    @pl.when(step == 0)
    def _():
        acc[...] = jnp.zeros_like(acc)

    def add(tile, picked, place):
        counts = cnt_ref[tile].astype(jnp.float32).astype(jnp.bfloat16)
        half_ref[place] = counts
        left = jnp.concatenate([picked, jnp.ones((rows - dim, side), jnp.bfloat16)], axis=0)
        product = lax.dot_general(
            left, counts, (((1,), (1,)), ((), ())), preferred_element_type=jnp.float32
        )
        dst = dst_ref[step * tiles + tile]
        acc[dst] += product

    @pl.when(step * tiles < slots)
    def _():
        for tile in range(tiles):
            slot = src_ref[step * tiles + tile] - blocks
            start = pl.multiple_of(lax.rem(slot, cap) * side, side)
            add(tile, recv_ref[lax.div(slot, cap), :, pl.ds(start, side)], slot)
            slot_dst_ref[slot] = dst_ref[step * tiles + tile]

    @pl.when(step * tiles >= slots)
    def _():
        for tile in range(tiles):
            start = pl.multiple_of(src_ref[step * tiles + tile] * side, side)
            add(tile, feat_ref[:, pl.ds(start, side)], step * tiles + tile)

    @pl.when(step == pl.num_programs(0) - 1)
    def _():
        per_part = agg_ref.shape[2] // side
        for block in range(blocks):
            part, at = block // per_part, (block % per_part) * side
            floor = jnp.maximum(acc[block, dim : dim + 1, :], 1.0)
            floor_ref[part, :, at : at + side] = floor
            agg_ref[part, :, at : at + side] = (acc[block, :dim, :] / floor).astype(jnp.bfloat16)


def swap_kernel(num_blk, num_col, src_ref, dst_ref, send_sem, recv_sem, own_sem):
    row, col, col_peer = positions(num_blk, num_col)
    greet(col_peer)
    copies = [
        push(src_ref.at[peer[1]], dst_ref.at[col], send_sem.at[step], recv_sem.at[step], peer)
        for step, peer in enumerate(col_peer)
    ]
    own = pltpu.make_async_copy(src_ref.at[col], dst_ref.at[col], own_sem)
    own.start()
    for copy in copies:
        copy.wait()
    own.wait()


def dense_kernel(
    chunk, feat_ref, agg_ref, cot_ref, floor_ref, ws_ref, wn_ref, bias_ref,
    *outs,
):
    scaled_refs, (self_ref, grad_ref, acc) = outs[:-3], outs[-3:]
    width, nodes = feat_ref.shape
    parts, _, piece, side = scaled_refs[0].shape
    dim = self_ref.shape[1]
    col = lax.axis_index("col")
    self_weight, neigh_weight = ws_ref[...], wn_ref[...]
    first = (((0,), (0,)), ((), ()))
    last = (((1,), (1,)), ((), ()))
    bias = bias_ref[...]
    for start in range(0, nodes, chunk):
        at = slice(start, start + chunk)
        feat, agg = feat_ref[:, at], agg_ref[:, at]
        pre_act = (
            lax.dot_general(self_weight, feat, first, preferred_element_type=jnp.float32)
            + lax.dot_general(neigh_weight, agg, first, preferred_element_type=jnp.float32)
            + bias
        )
        dz = (cot_ref[:, at].astype(jnp.float32) * gelu_slope(pre_act)).astype(jnp.bfloat16)
        floor = floor_ref[col, :, at]
        neigh = jnp.dot(neigh_weight, dz, preferred_element_type=jnp.float32) / floor
        own = jnp.dot(self_weight, dz, preferred_element_type=jnp.float32)
        for part in range(parts):
            rows = slice(part * dim, (part + 1) * dim)
            for index, scaled_ref in enumerate(scaled_refs):
                top = part * dim + index * piece
                for left in range(0, chunk, side):
                    scaled_ref[part, (start + left) // side] = neigh[
                        top : top + piece, left : left + side
                    ].astype(jnp.bfloat16)
            self_ref[part, :, at] = own[rows].astype(jnp.bfloat16)
        ones = jnp.ones((16, chunk), jnp.bfloat16)
        left = jnp.concatenate([feat, agg, ones], axis=0)
        grads = lax.dot_general(left, dz, last, preferred_element_type=jnp.float32)
        if start == 0:
            acc[...] = grads
        else:
            acc[...] += grads
    for part in range(parts):
        rows = slice(part * dim, (part + 1) * dim)
        grad_ref[part, :dim, :width] = acc[rows, :].astype(jnp.bfloat16)
        grad_ref[part, dim:, :width] = acc[width + part * dim : width + (part + 1) * dim, :].astype(
            jnp.bfloat16
        )
        bias_row = acc[2 * width : 2 * width + 1, rows].astype(jnp.bfloat16)
        grad_ref[part, :, width : width + dim] = jnp.broadcast_to(bias_row, (2 * dim, dim))
        if dim < grad_ref.shape[2] - width:
            rest = grad_ref.shape[2] - width - dim
            grad_ref[part, :, width + dim :] = jnp.zeros((2 * dim, rest), jnp.bfloat16)


def return_kernel(
    num_blk, num_col, slot_dst, half_ref, scaled_a, scaled_b, self_ref, grad_ref,
    all_a, all_b, came_ref, self_all, grad_out, bias_out,
    ret, core_buf, mid_src, mid_buf, far_src, far_buf, side_src, side_buf,
    halo_send, halo_recv, col_send, col_recv, core_send, core_recv, mid_send, mid_recv,
    far_send, far_recv, down_send, down_recv, own_sem,
):
    slots = ret.shape[1]
    num_hops = halo_send.shape[1]
    cap = slots // num_hops
    blocks = scaled_a.shape[1]
    row, col, col_peer = positions(num_blk, num_col)
    far_size = num_blk // 4
    core, mid, far = row % 2, (row // 2) % 2, row // 4
    width = grad_out.shape[4]
    halo = halo_peers(row, col, num_blk, num_hops, -1)
    core_peer = (far * 4 + mid * 2 + 1 - core, col)
    mid_peer = (far * 4 + (1 - mid) * 2 + core, col)
    far_peers = [((far + step) % far_size * 4 + mid * 2 + core, col) for step in range(1, far_size)]
    cross_peer = (far * 4 + (1 - mid) * 2 + 1 - core, col)
    greet(halo + [core_peer, mid_peer, cross_peer] + far_peers + col_peer)

    def across(at, source, target):
        return [
            push(source.at[peer[1]], target(step), col_send.at[at, step], col_recv.at[at, step], peer)
            for step, peer in enumerate(col_peer)
        ]

    def settle(copies):
        for copy in copies:
            copy.wait()

    mine = pl.ds(col * blocks, blocks)
    owns = []
    for at, (source, target) in enumerate(
        ((scaled_a.at[col], all_a.at[mine]), (scaled_b.at[col], all_b.at[mine]), (self_ref.at[col], self_all.at[col]))
    ):
        own = pltpu.make_async_copy(source, target, own_sem.at[at])
        own.start()
        owns.append(own)
    first = across(1, scaled_a, lambda step: all_a.at[mine])
    ups = [
        push(grad_ref.at[part, 1 - core], core_buf.at[part], core_send.at[part], core_recv.at[part], core_peer)
        for part in range(num_col)
    ]

    def spread(index, source):
        def body(slot, carry):
            picked = source[slot_dst[slot]]
            ret[index, slot] = jnp.dot(
                picked, half_ref[slot], preferred_element_type=jnp.float32
            ).astype(jnp.bfloat16)
            return carry

        lax.fori_loop(0, slots, body, 0, unroll=8)

    def give(index):
        copies = []
        for at in range(num_hops):
            part = pl.ds(at * cap, cap)
            copies.append(
                push(
                    ret.at[index, part], came_ref.at[index, part], halo_send.at[index, at],
                    halo_recv.at[index, at], halo[at],
                )
            )
        return copies

    settle(ups)
    for part in range(num_col):
        mid_src[part] = added(grad_ref[part, core], core_buf[part]).astype(jnp.bfloat16)
    ups = [
        push(mid_src.at[part, 1 - mid], mid_buf.at[part], mid_send.at[part], mid_recv.at[part], mid_peer)
        for part in range(num_col)
    ]
    settle(first)
    second = across(2, scaled_b, lambda step: all_b.at[mine])
    owns[0].wait()
    spread(0, all_a)
    settle(ups)
    for part in range(num_col):
        far_src[:, part] = added(mid_src[part, mid], mid_buf[part]).astype(jnp.bfloat16)
    ups = [
        push(far_src.at[peer[0] // 4], far_buf.at[step], far_send.at[step], far_recv.at[step], peer)
        for step, peer in enumerate(far_peers)
    ]
    later = give(0)
    settle(second)
    owns[1].wait()
    spread(1, all_b)
    later += give(1)
    settle(ups)
    total = far_src[far].astype(jnp.float32)
    for step in range(far_size - 1):
        total += far_buf[step].astype(jnp.float32)
    side_src[...] = total.astype(jnp.bfloat16)
    ups = across(0, side_src, lambda step: side_buf.at[step])
    later += across(3, self_ref, lambda step: self_all.at[col])
    settle(ups)
    total = side_src[col].astype(jnp.float32)
    for step in range(num_col - 1):
        total += side_buf[step].astype(jnp.float32)
    bias_out[...] = total[0:1, width:]
    grad_out[core, mid, far] = total[:, :width].astype(jnp.bfloat16)
    settle([
        push(
            grad_out.at[core, mid, far], grad_out.at[core, mid, far], down_send.at[3 + step],
            down_recv.at[3 + step], peer,
        )
        for step, peer in enumerate(far_peers)
    ])
    settle([
        push(grad_out.at[core, mid], grad_out.at[core, mid], down_send.at[at], down_recv.at[at], peer)
        for at, peer in enumerate((core_peer, mid_peer, cross_peer))
    ])
    settle(later)
    owns[2].wait()


def finish_kernel(
    slots, send_ref, dst_ref, src_ref, half_ref, all_a, all_b, self_ref, came_ref, out_ref, acc
):
    blocks, _, side = acc.shape
    num_hops, cap = send_ref.shape[1:]
    piece = all_a.shape[1]
    acc[...] = jnp.zeros_like(acc)
    for tile in range(slots, dst_ref.shape[0]):
        dst = dst_ref[tile]
        picked = jnp.concatenate([all_a[dst], all_b[dst]], axis=0)
        acc[src_ref[tile]] += jnp.dot(picked, half_ref[tile], preferred_element_type=jnp.float32)
    for slot in range(slots):
        came = jnp.concatenate([came_ref[0, slot], came_ref[1, slot]], axis=0)
        acc[send_ref[0, slot // cap, slot % cap]] += came.astype(jnp.float32)
    per_part = self_ref.shape[2] // side
    for block in range(blocks):
        at = (block % per_part) * side
        own = self_ref[block // per_part, :, at : at + side].astype(jnp.float32)
        out_ref[:, block * side : (block + 1) * side] = (acc[block] + own).astype(jnp.bfloat16)


def per_device(
    num_blk, num_col,
    node_feats, tile_dst, tile_src, tile_cnt, send_blk, self_weight, neigh_weight, bias, cotangent,
):
    half, full = jnp.bfloat16, jnp.float32
    dim, rows = node_feats.shape
    tiles, side, _ = tile_cnt.shape
    blocks = rows // side
    num_hops, cap = send_blk.shape[1:]
    slots = num_hops * cap
    part = rows // num_col
    width = self_weight.shape[0]
    dma = pltpu.SemaphoreType.DMA
    shape = jax.ShapeDtypeStruct
    peers = max(num_col - 1, 1)
    split = shape((num_col, dim, part), half)
    slot_shape = shape((num_hops, dim, cap * side), half)

    outgoing = pl.pallas_call(
        pack_kernel,
        out_shape=slot_shape,
        in_specs=[smem(), vmem()],
        out_specs=vmem(),
        compiler_params=params(),
        name="pack",
    )(send_blk, node_feats)
    received, feat_all, cot_all = pl.pallas_call(
        functools.partial(halo_kernel, num_blk, num_col),
        out_shape=(slot_shape, split, split),
        in_specs=[anywhere()] * 3,
        out_specs=(anywhere(),) * 3,
        scratch_shapes=[
            dma((num_hops,)), dma((num_hops,)), dma((2, peers)), dma((2, peers)), dma((2,)),
        ],
        compiler_params=params(0),
        name="halo",
    )(outgoing, node_feats, cotangent)

    steps = tiles // STEP_TILES
    cnt_spec = pl.BlockSpec((STEP_TILES, side, side), lambda step: (step, 0, 0))
    whole = lambda dims: pl.BlockSpec(dims, lambda step: (0,) * len(dims))
    aggregate, floor, half_cnt, slot_dst = pl.pallas_call(
        functools.partial(aggregate_kernel, slots),
        grid=(steps,),
        out_shape=(
            split, shape((num_col, 1, part), full), shape((tiles, side, side), half),
            shape((slots,), jnp.int32),
        ),
        in_specs=[smem(), smem(), whole((dim, rows)), whole(slot_shape.shape), cnt_spec],
        out_specs=(whole(split.shape), whole((num_col, 1, part)), whole((tiles, side, side)), smem()),
        scratch_shapes=[pltpu.VMEM((blocks, dim + 16, side), full)],
        compiler_params=params(),
        name="aggregate",
    )(tile_dst, tile_src, node_feats, received, tile_cnt)

    def swap(array, collective, name):
        return pl.pallas_call(
            functools.partial(swap_kernel, num_blk, num_col),
            out_shape=split,
            in_specs=[anywhere()],
            out_specs=anywhere(),
            scratch_shapes=[dma((peers,)), dma((peers,)), dma(())],
            compiler_params=params(collective),
            name=name,
        )(array)

    agg_all = swap(aggregate, 1, "swap_aggregate")
    lanes = width + 128
    per_part = part // side
    piece = dim // 2
    scaled_shape = shape((num_col, per_part, piece, side), half)
    scaled_a, scaled_b, own_part, grads = pl.pallas_call(
        functools.partial(dense_kernel, min(part, 256)),
        out_shape=(scaled_shape, scaled_shape, split, shape((num_col, 2 * dim, lanes), half)),
        in_specs=[vmem()] * 7,
        out_specs=(vmem(),) * 4,
        scratch_shapes=[pltpu.VMEM((2 * width + 16, width), full)],
        compiler_params=params(),
        name="dense",
    )(
        feat_all.reshape(width, part), agg_all.reshape(width, part), cot_all.reshape(width, part),
        floor, self_weight, neigh_weight, bias.reshape(width, 1),
    )

    far_size = num_blk // 4
    span = 2 * dim // num_blk
    all_shape = shape((blocks, piece, side), half)
    level = lambda *lead: pltpu.VMEM(lead + (span, lanes), half)
    all_a, all_b, came, own_all, grad_sum, bias_sum = pl.pallas_call(
        functools.partial(return_kernel, num_blk, num_col),
        out_shape=(
            all_shape, all_shape, shape((2, slots, piece, side), half), split,
            shape((2, 2, far_size, span, width), half), shape((1, 128), full),
        ),
        in_specs=[smem()] + [vmem()] * 5,
        out_specs=(vmem(),) * 6,
        scratch_shapes=[
            pltpu.VMEM((2, slots, piece, side), half),
            level(num_col, 2, far_size), level(num_col, 2, far_size), level(num_col, far_size),
            level(far_size, num_col), level(max(far_size - 1, 1), num_col), level(num_col), level(peers),
            dma((2, num_hops)), dma((2, num_hops)), dma((4, peers)), dma((4, peers)),
            dma((num_col,)), dma((num_col,)), dma((num_col,)), dma((num_col,)),
            dma((far_size,)), dma((far_size,)), dma((far_size + 2,)), dma((far_size + 2,)),
            dma((3,)),
        ],
        compiler_params=params(2),
        name="give_back",
    )(
        slot_dst, half_cnt, scaled_a, scaled_b, own_part,
        grads.reshape(num_col, 2, 2, far_size, span, lanes),
    )

    grad_feats = pl.pallas_call(
        functools.partial(finish_kernel, slots),
        out_shape=shape((dim, rows), half),
        in_specs=[smem()] * 3 + [vmem()] * 5,
        out_specs=vmem(),
        scratch_shapes=[pltpu.VMEM((blocks, dim, side), full)],
        compiler_params=params(),
        name="finish",
    )(send_blk, tile_dst, tile_src, half_cnt, all_a, all_b, own_all, came)
    grad_both = grad_sum.reshape(2 * dim, width).astype(full)
    return (grad_feats, grad_both[:dim], grad_both[dim:], bias_sum[0, :dim])


def solution(mesh):
    placed = (
        P("col", "blk"),
        P("blk"),
        P("blk"),
        P("blk", None, None),
        P("blk", None, None),
        P(),
        P(),
        P(),
        P("col", "blk"),
    )
    return jax.shard_map(
        functools.partial(per_device, mesh.shape["blk"], mesh.shape["col"]),
        mesh=mesh,
        in_specs=placed,
        out_specs=(P("col", "blk"), P("col", None), P("col", None), P("col")),
        check_vma=False,
    )
```

```python
import functools

import jax
import jax.numpy as jnp
from jax import lax
from jax.experimental import pallas as pl
from jax.experimental.pallas import tpu as pltpu
from jax.sharding import PartitionSpec as P

MESH = pl.DeviceIdType.MESH
VMEM_BYTES = 40 * 1024 * 1024


def gelu_slope(pre_act):
    inner = 0.7978845608 * (pre_act + 0.044715 * pre_act * pre_act * pre_act)
    tanh_value = jnp.tanh(inner)
    return 0.5 * (1.0 + tanh_value) + 0.5 * pre_act * (
        1.0 - tanh_value * tanh_value
    ) * 0.7978845608 * (1.0 + 3.0 * 0.044715 * pre_act * pre_act)


def hop(index):
    return (index // 2 + 1) * (1 - 2 * (index % 2))


def vmem():
    return pl.BlockSpec(memory_space=pltpu.VMEM)


def smem():
    return pl.BlockSpec(memory_space=pltpu.SMEM)


def anywhere():
    return pl.BlockSpec(memory_space=pl.ANY)


def params(collective=None, vmem_bytes=VMEM_BYTES):
    if collective is None:
        return pltpu.CompilerParams(vmem_limit_bytes=vmem_bytes)
    return pltpu.CompilerParams(
        vmem_limit_bytes=vmem_bytes, collective_id=collective, has_side_effects=True
    )


def added(one, other):
    return one.astype(jnp.float32) + other.astype(jnp.float32)


def positions(num_blk, num_col):
    row, col = lax.axis_index("blk"), lax.axis_index("col")
    col_peer = [(row, lax.rem(col + step, num_col)) for step in range(1, num_col)]
    return row, col, col_peer


def greet(peers):
    barrier = pltpu.get_barrier_semaphore()
    for peer in peers:
        pl.semaphore_signal(barrier, inc=1, device_id=peer, device_id_type=MESH)
    pl.semaphore_wait(barrier, len(peers))


def push(src, dst, send_sem, recv_sem, peer):
    copy = pltpu.make_async_remote_copy(
        src_ref=src,
        dst_ref=dst,
        send_sem=send_sem,
        recv_sem=recv_sem,
        device_id=peer,
        device_id_type=MESH,
    )
    copy.start()
    return copy


def halo_peers(row, col, num_blk, num_hops, sign):
    return [
        (lax.rem(row + sign * hop(index) + num_blk, num_blk), col) for index in range(num_hops)
    ]


def pack_kernel(
    send_ref, dst_ref, src_ref, feat_ref, out_ref, local_ref, tile_of, prev_ref, last_ref, slot_dst
):
    slots, piece, side = out_ref.shape[1:]
    cap = send_ref.shape[2]
    blocks = last_ref.shape[0]
    locals_ = local_ref.shape[0]
    for slot in range(slots):
        start = pl.multiple_of(send_ref[0, slot // cap, slot % cap] * side, side)
        picked = feat_ref[:, pl.ds(start, side)]
        out_ref[0, slot] = picked[:piece]
        out_ref[1, slot] = picked[piece:]
    for at in range(locals_):
        start = pl.multiple_of(src_ref[slots + at] * side, side)
        local_ref[at] = feat_ref[:, pl.ds(start, side)]
    for block in range(blocks):
        last_ref[block] = 0

    def link(at, dst):
        prev_ref[at] = last_ref[dst]
        last_ref[dst] = at + 1

    def local_step(at, carry):
        link(at, dst_ref[slots + at])
        return carry

    def find_step(tile, carry):
        tile_of[src_ref[tile] - blocks] = tile
        return carry

    def slot_step(slot, carry):
        dst = dst_ref[tile_of[slot]]
        slot_dst[slot] = dst
        link(locals_ + slot, dst)
        return carry

    lax.fori_loop(0, locals_, local_step, 0)
    lax.fori_loop(0, slots, find_step, 0)
    lax.fori_loop(0, slots, slot_step, 0)


def gather_kernel(
    num_blk, num_col, tile_of, prev_ref, last_ref, sbuf, local_ref, feat_ref, cot_ref, cnt_hbm,
    feat_all, cot_all, all_a, all_b, floor_ref, half_ref,
    recv, sum_a, sum_b, sum_d, agg_src, cnt_ref,
    halo_send, halo_recv, col_send, col_recv, own_sem, cnt_sem,
):
    slots, piece, side = sbuf.shape[1:]
    num_hops = halo_send.shape[1]
    cap = slots // num_hops
    part = feat_all.shape[2]
    dim = 2 * piece
    locals_ = local_ref.shape[0]
    blocks = last_ref.shape[0]
    per_part = part // side
    row, col, col_peer = positions(num_blk, num_col)
    halo = halo_peers(row, col, num_blk, num_hops, 1)
    counts_in = pltpu.make_async_copy(cnt_hbm, cnt_ref, cnt_sem)
    counts_in.start()
    greet(halo + col_peer)
    halves = []
    for index in range(2):
        copies = []
        for at in range(num_hops):
            some = pl.ds(at * cap, cap)
            copies.append(
                push(
                    sbuf.at[index, some], recv.at[index, some], halo_send.at[index, at],
                    halo_recv.at[index, at], halo[at],
                )
            )
        halves.append(copies)
    later = []

    def share(at, pick, target):
        for step, peer in enumerate(col_peer):
            later.append(push(pick(peer[1]), target.at[col], col_send.at[at, step], col_recv.at[at, step], peer))
        own = pltpu.make_async_copy(pick(col), target.at[col], own_sem.at[at])
        own.start()
        later.append(own)

    def nodes_of(source):
        return lambda index: source.at[:, pl.ds(pl.multiple_of(index * part, part), part)]

    share(0, nodes_of(feat_ref), feat_all)
    share(1, nodes_of(cot_ref), cot_all)
    ones = jnp.ones((16, side), jnp.bfloat16)
    for total in (sum_a, sum_b, sum_d):
        total[0] = jnp.zeros(total.shape[1:], jnp.float32)
    counts_in.wait()

    def times(left, counts):
        return lax.dot_general(left, counts, (((1,), (1,)), ((), ())), preferred_element_type=jnp.float32)

    def local_step(at, carry):
        counts = cnt_ref[slots + at].astype(jnp.float32).astype(jnp.bfloat16)
        half_ref[slots + at] = counts
        product = times(jnp.concatenate([local_ref[at], ones], axis=0), counts)
        before = prev_ref[at]
        sum_a[at + 1] = sum_a[before] + product[:piece]
        sum_b[at + 1] = sum_b[before] + product[piece:dim]
        sum_d[at + 1] = sum_d[before] + product[dim:]
        return carry

    def first_step(slot, carry):
        counts = cnt_ref[tile_of[slot]].astype(jnp.float32).astype(jnp.bfloat16)
        half_ref[slot] = counts
        product = times(jnp.concatenate([recv[0, slot], ones], axis=0), counts)
        before = prev_ref[locals_ + slot]
        sum_a[locals_ + slot + 1] = sum_a[before] + product[:piece]
        sum_d[locals_ + slot + 1] = sum_d[before] + product[piece:]
        return carry

    def second_step(slot, carry):
        before = prev_ref[locals_ + slot]
        sum_b[locals_ + slot + 1] = sum_b[before] + times(recv[1, slot], half_ref[slot])
        return carry

    lax.fori_loop(0, locals_, local_step, 0, unroll=4)
    for index, (step, total, target) in enumerate(
        ((first_step, sum_a, all_a), (second_step, sum_b, all_b))
    ):
        for at, copy in enumerate(halves[index]):
            copy.wait()
            lax.fori_loop(at * cap, (at + 1) * cap, step, 0, unroll=True)
        for block in range(blocks):
            last = last_ref[block]
            group, left = block // per_part, (block % per_part) * side
            floor = jnp.maximum(sum_d[last][0:1], 1.0)
            if index == 0:
                floor_ref[group, :, left : left + side] = floor
            agg_src[index, group, :, left : left + side] = (total[last] / floor).astype(jnp.bfloat16)
        share(2 + index, lambda where: agg_src.at[index, where], target)
    for copy in later:
        copy.wait()


def dense_kernel(
    chunk, feat_ref, agg_a, agg_b, cot_ref, floor_ref, ws_ref, wn_ref, bias_ref,
    *outs,
):
    scaled_refs, (self_ref, grad_ref, acc) = outs[:-3], outs[-3:]
    width, nodes = feat_ref.shape
    parts, _, piece, side = scaled_refs[0].shape
    dim = self_ref.shape[1]
    col = lax.axis_index("col")
    self_weight, neigh_weight = ws_ref[...], wn_ref[...]
    first = (((0,), (0,)), ((), ()))
    last = (((1,), (1,)), ((), ()))
    bias = jnp.transpose(jnp.broadcast_to(bias_ref[...], (8, width)))[:, 0:1]
    for start in range(0, nodes, chunk):
        at = slice(start, start + chunk)
        feat = feat_ref[:, at]
        agg = jnp.concatenate(
            [half[part, :, at] for part in range(parts) for half in (agg_a, agg_b)], axis=0
        )
        pre_act = (
            lax.dot_general(self_weight, feat, first, preferred_element_type=jnp.float32)
            + lax.dot_general(neigh_weight, agg, first, preferred_element_type=jnp.float32)
            + bias
        )
        dz = (cot_ref[:, at].astype(jnp.float32) * gelu_slope(pre_act)).astype(jnp.bfloat16)
        floor = floor_ref[col, :, at]
        neigh = jnp.dot(neigh_weight, dz, preferred_element_type=jnp.float32) / floor
        own = jnp.dot(self_weight, dz, preferred_element_type=jnp.float32)
        for part in range(parts):
            rows = slice(part * dim, (part + 1) * dim)
            for index, scaled_ref in enumerate(scaled_refs):
                top = part * dim + index * piece
                for left in range(0, chunk, side):
                    scaled_ref[part, (start + left) // side] = neigh[
                        top : top + piece, left : left + side
                    ].astype(jnp.bfloat16)
            self_ref[part, :, at] = own[rows].astype(jnp.bfloat16)
        ones = jnp.ones((16, chunk), jnp.bfloat16)
        left = jnp.concatenate([feat, agg, ones], axis=0)
        grads = lax.dot_general(left, dz, last, preferred_element_type=jnp.float32)
        if start == 0:
            acc[...] = grads
        else:
            acc[...] += grads
    for part in range(parts):
        rows = slice(part * dim, (part + 1) * dim)
        grad_ref[part, :dim, :width] = acc[rows, :].astype(jnp.bfloat16)
        grad_ref[part, dim:, :width] = acc[width + part * dim : width + (part + 1) * dim, :].astype(
            jnp.bfloat16
        )
        bias_row = acc[2 * width : 2 * width + 1, rows].astype(jnp.bfloat16)
        grad_ref[part, :, width : width + dim] = jnp.broadcast_to(bias_row, (2 * dim, dim))
        if dim < grad_ref.shape[2] - width:
            rest = grad_ref.shape[2] - width - dim
            grad_ref[part, :, width + dim :] = jnp.zeros((2 * dim, rest), jnp.bfloat16)


def return_kernel(
    num_blk, num_col, slot_dst, half_ref, scaled_a, scaled_b, self_ref, grad_ref,
    all_a, all_b, came_ref, self_all, grad_out, bias_out,
    ret, core_buf, mid_src, mid_buf, far_src, far_buf, side_src, side_buf,
    halo_send, halo_recv, col_send, col_recv, core_send, core_recv, mid_send, mid_recv,
    far_send, far_recv, down_send, down_recv, own_sem,
):
    slots = ret.shape[1]
    num_hops = halo_send.shape[1]
    cap = slots // num_hops
    blocks = scaled_a.shape[1]
    row, col, col_peer = positions(num_blk, num_col)
    far_size = num_blk // 4
    core, mid, far = row % 2, (row // 2) % 2, row // 4
    width = grad_out.shape[4]
    halo = halo_peers(row, col, num_blk, num_hops, -1)
    core_peer = (far * 4 + mid * 2 + 1 - core, col)
    mid_peer = (far * 4 + (1 - mid) * 2 + core, col)
    far_peers = [((far + step) % far_size * 4 + mid * 2 + core, col) for step in range(1, far_size)]
    cross_peer = (far * 4 + (1 - mid) * 2 + 1 - core, col)
    greet(halo + [core_peer, mid_peer, cross_peer] + far_peers + col_peer)

    def across(at, source, target):
        return [
            push(source.at[peer[1]], target(step), col_send.at[at, step], col_recv.at[at, step], peer)
            for step, peer in enumerate(col_peer)
        ]

    def settle(copies):
        for copy in copies:
            copy.wait()

    mine = pl.ds(col * blocks, blocks)
    owns = []
    for at, (source, target) in enumerate(
        ((scaled_a.at[col], all_a.at[mine]), (scaled_b.at[col], all_b.at[mine]), (self_ref.at[col], self_all.at[col]))
    ):
        own = pltpu.make_async_copy(source, target, own_sem.at[at])
        own.start()
        owns.append(own)
    first = across(1, scaled_a, lambda step: all_a.at[mine])
    ups = [
        push(grad_ref.at[part, 1 - core], core_buf.at[part], core_send.at[part], core_recv.at[part], core_peer)
        for part in range(num_col)
    ]

    def spread(index, source):
        def body(slot, carry):
            picked = source[slot_dst[slot]]
            ret[index, slot] = jnp.dot(
                picked, half_ref[slot], preferred_element_type=jnp.float32
            ).astype(jnp.bfloat16)
            return carry

        lax.fori_loop(0, slots, body, 0, unroll=8)

    def give(index):
        copies = []
        for at in range(num_hops):
            part = pl.ds(at * cap, cap)
            copies.append(
                push(
                    ret.at[index, part], came_ref.at[index, part], halo_send.at[index, at],
                    halo_recv.at[index, at], halo[at],
                )
            )
        return copies

    settle(ups)
    for part in range(num_col):
        mid_src[part] = added(grad_ref[part, core], core_buf[part]).astype(jnp.bfloat16)
    ups = [
        push(mid_src.at[part, 1 - mid], mid_buf.at[part], mid_send.at[part], mid_recv.at[part], mid_peer)
        for part in range(num_col)
    ]
    settle(first)
    second = across(2, scaled_b, lambda step: all_b.at[mine])
    owns[0].wait()
    spread(0, all_a)
    settle(ups)
    for part in range(num_col):
        far_src[:, part] = added(mid_src[part, mid], mid_buf[part]).astype(jnp.bfloat16)
    ups = [
        push(far_src.at[peer[0] // 4], far_buf.at[step], far_send.at[step], far_recv.at[step], peer)
        for step, peer in enumerate(far_peers)
    ]
    later = give(0)
    settle(second)
    owns[1].wait()
    spread(1, all_b)
    settle(ups)
    total = far_src[far].astype(jnp.float32)
    for step in range(far_size - 1):
        total += far_buf[step].astype(jnp.float32)
    side_src[...] = total.astype(jnp.bfloat16)
    ups = across(0, side_src, lambda step: side_buf.at[step])
    later += across(3, self_ref, lambda step: self_all.at[col])
    settle(ups)
    total = side_src[col].astype(jnp.float32)
    for step in range(num_col - 1):
        total += side_buf[step].astype(jnp.float32)
    bias_out[...] = total[0:1, width:]
    grad_out[core, mid, far] = total[:, :width].astype(jnp.bfloat16)
    downs = [
        push(
            grad_out.at[core, mid, far], grad_out.at[core, mid, far], down_send.at[3 + step],
            down_recv.at[3 + step], peer,
        )
        for step, peer in enumerate(far_peers)
    ]
    later += give(1)
    settle(downs)
    settle([
        push(grad_out.at[core, mid], grad_out.at[core, mid], down_send.at[at], down_recv.at[at], peer)
        for at, peer in enumerate((core_peer, mid_peer, cross_peer))
    ])
    settle(later)
    owns[2].wait()


def finish_kernel(
    slots, send_ref, dst_ref, src_ref, half_ref, all_a, all_b, self_ref, came_ref, grad_ref, bias_ref,
    out_ref, grad_self, grad_neigh, grad_bias, acc,
):
    blocks, _, side = acc.shape
    num_hops, cap = send_ref.shape[1:]
    piece = all_a.shape[1]
    dim = grad_self.shape[0]
    grad_self[...] = grad_ref[:dim].astype(jnp.float32)
    grad_neigh[...] = grad_ref[dim:].astype(jnp.float32)
    grad_bias[...] = bias_ref[:, :dim]
    acc[...] = jnp.zeros_like(acc)
    for tile in range(slots, dst_ref.shape[0]):
        dst = dst_ref[tile]
        picked = jnp.concatenate([all_a[dst], all_b[dst]], axis=0)
        acc[src_ref[tile]] += jnp.dot(picked, half_ref[tile], preferred_element_type=jnp.float32)
    for slot in range(slots):
        came = jnp.concatenate([came_ref[0, slot], came_ref[1, slot]], axis=0)
        acc[send_ref[0, slot // cap, slot % cap]] += came.astype(jnp.float32)
    per_part = self_ref.shape[2] // side
    for block in range(blocks):
        at = (block % per_part) * side
        own = self_ref[block // per_part, :, at : at + side].astype(jnp.float32)
        out_ref[:, block * side : (block + 1) * side] = (acc[block] + own).astype(jnp.bfloat16)


def per_device(
    num_blk, num_col,
    node_feats, tile_dst, tile_src, tile_cnt, send_blk, self_weight, neigh_weight, bias, cotangent,
):
    half, full = jnp.bfloat16, jnp.float32
    dim, rows = node_feats.shape
    tiles, side, _ = tile_cnt.shape
    blocks = rows // side
    num_hops, cap = send_blk.shape[1:]
    slots = num_hops * cap
    part = rows // num_col
    width = self_weight.shape[0]
    dma = pltpu.SemaphoreType.DMA
    shape = jax.ShapeDtypeStruct
    peers = max(num_col - 1, 1)
    split = shape((num_col, dim, part), half)
    locals_ = tiles - slots
    piece = dim // 2
    slot_shape = shape((2, slots, piece, side), half)
    ints = lambda count: shape((count,), jnp.int32)

    outgoing, local_src, tile_of, prev, last, slot_dst = pl.pallas_call(
        pack_kernel,
        out_shape=(
            slot_shape, shape((locals_, dim, side), half), ints(slots), ints(tiles), ints(blocks), ints(slots),
        ),
        in_specs=[smem()] * 3 + [vmem()],
        out_specs=(vmem(), vmem()) + (smem(),) * 4,
        compiler_params=params(),
        name="pack",
    )(send_blk, tile_dst, tile_src, node_feats)
    agg_shape = shape((num_col, piece, part), half)
    hbm = pl.BlockSpec(memory_space=pltpu.HBM)
    sums = lambda count: pltpu.VMEM((tiles + 1, count, side), full)
    feat_all, cot_all, agg_a, agg_b, floor, half_cnt = pl.pallas_call(
        functools.partial(gather_kernel, num_blk, num_col),
        out_shape=(
            split, split, agg_shape, agg_shape, shape((num_col, 1, part), full), shape((tiles, side, side), half),
        ),
        in_specs=[smem()] * 3 + [vmem()] * 2 + [hbm] * 3,
        out_specs=(vmem(),) * 6,
        scratch_shapes=[
            pltpu.VMEM(slot_shape.shape, half), sums(piece), sums(piece), sums(16),
            pltpu.VMEM((2, num_col, piece, part), half), pltpu.VMEM((tiles, side, side), jnp.int32),
            dma((2, num_hops)), dma((2, num_hops)), dma((4, peers)), dma((4, peers)), dma((4,)), dma(()),
        ],
        compiler_params=params(0, 56 * 1024 * 1024),
        name="gather",
    )(tile_of, prev, last, outgoing, local_src, node_feats, cotangent, tile_cnt)

    lanes = width + 128
    per_part = part // side
    scaled_shape = shape((num_col, per_part, piece, side), half)
    scaled_a, scaled_b, own_part, grads = pl.pallas_call(
        functools.partial(dense_kernel, min(part, 256)),
        out_shape=(scaled_shape, scaled_shape, split, shape((num_col, 2 * dim, lanes), half)),
        in_specs=[vmem()] * 8,
        out_specs=(vmem(),) * 4,
        scratch_shapes=[pltpu.VMEM((2 * width + 16, width), full)],
        compiler_params=params(),
        name="dense",
    )(
        feat_all.reshape(width, part), agg_a, agg_b, cot_all.reshape(width, part),
        floor, self_weight, neigh_weight, bias.reshape(1, width),
    )

    far_size = num_blk // 4
    span = 2 * dim // num_blk
    all_shape = shape((blocks, piece, side), half)
    level = lambda *lead: pltpu.VMEM(lead + (span, lanes), half)
    all_a, all_b, came, own_all, grad_sum, bias_sum = pl.pallas_call(
        functools.partial(return_kernel, num_blk, num_col),
        out_shape=(
            all_shape, all_shape, shape((2, slots, piece, side), half), split,
            shape((2, 2, far_size, span, width), half), shape((1, 128), full),
        ),
        in_specs=[smem()] + [vmem()] * 5,
        out_specs=(vmem(),) * 6,
        scratch_shapes=[
            pltpu.VMEM((2, slots, piece, side), half),
            level(num_col, 2, far_size), level(num_col, 2, far_size), level(num_col, far_size),
            level(far_size, num_col), level(max(far_size - 1, 1), num_col), level(num_col), level(peers),
            dma((2, num_hops)), dma((2, num_hops)), dma((4, peers)), dma((4, peers)),
            dma((num_col,)), dma((num_col,)), dma((num_col,)), dma((num_col,)),
            dma((far_size,)), dma((far_size,)), dma((far_size + 2,)), dma((far_size + 2,)),
            dma((3,)),
        ],
        compiler_params=params(2),
        name="give_back",
    )(
        slot_dst, half_cnt, scaled_a, scaled_b, own_part,
        grads.reshape(num_col, 2, 2, far_size, span, lanes),
    )

    weight_shape = shape((dim, width), full)
    grad_feats, grad_self, grad_neigh, grad_bias = pl.pallas_call(
        functools.partial(finish_kernel, slots),
        out_shape=(shape((dim, rows), half), weight_shape, weight_shape, shape((1, dim), full)),
        in_specs=[smem()] * 3 + [vmem()] * 7,
        out_specs=(vmem(),) * 4,
        scratch_shapes=[pltpu.VMEM((blocks, dim, side), full)],
        compiler_params=params(),
        name="finish",
    )(
        send_blk, tile_dst, tile_src, half_cnt, all_a, all_b, own_all, came,
        grad_sum.reshape(2 * dim, width), bias_sum,
    )
    return (grad_feats, grad_self, grad_neigh, grad_bias.reshape(dim))


def solution(mesh):
    placed = (
        P("col", "blk"),
        P("blk"),
        P("blk"),
        P("blk", None, None),
        P("blk", None, None),
        P(),
        P(),
        P(),
        P("col", "blk"),
    )
    return jax.shard_map(
        functools.partial(per_device, mesh.shape["blk"], mesh.shape["col"]),
        mesh=mesh,
        in_specs=placed,
        out_specs=(P("col", "blk"), P("col", None), P("col", None), P("col")),
        check_vma=False,
    )
```

```python
import functools

import jax
import jax.numpy as jnp
from jax import lax
from jax.experimental import pallas as pl
from jax.experimental.pallas import tpu as pltpu
from jax.sharding import PartitionSpec as P

MESH = pl.DeviceIdType.MESH
VMEM_BYTES = 40 * 1024 * 1024


def gelu_slope(pre_act):
    inner = 0.7978845608 * (pre_act + 0.044715 * pre_act * pre_act * pre_act)
    tanh_value = jnp.tanh(inner)
    return 0.5 * (1.0 + tanh_value) + 0.5 * pre_act * (
        1.0 - tanh_value * tanh_value
    ) * 0.7978845608 * (1.0 + 3.0 * 0.044715 * pre_act * pre_act)


def hop(index):
    return (index // 2 + 1) * (1 - 2 * (index % 2))


def vmem():
    return pl.BlockSpec(memory_space=pltpu.VMEM)


def smem():
    return pl.BlockSpec(memory_space=pltpu.SMEM)


def anywhere():
    return pl.BlockSpec(memory_space=pl.ANY)


def params(collective=None, vmem_bytes=VMEM_BYTES):
    if collective is None:
        return pltpu.CompilerParams(vmem_limit_bytes=vmem_bytes)
    return pltpu.CompilerParams(
        vmem_limit_bytes=vmem_bytes, collective_id=collective, has_side_effects=True
    )


def added(one, other):
    return one.astype(jnp.float32) + other.astype(jnp.float32)


def positions(num_blk, num_col):
    row, col = lax.axis_index("blk"), lax.axis_index("col")
    col_peer = [(row, lax.rem(col + step, num_col)) for step in range(1, num_col)]
    return row, col, col_peer


def greet(peers):
    barrier = pltpu.get_barrier_semaphore()
    for peer in peers:
        pl.semaphore_signal(barrier, inc=1, device_id=peer, device_id_type=MESH)
    pl.semaphore_wait(barrier, len(peers))


def push(src, dst, send_sem, recv_sem, peer):
    copy = pltpu.make_async_remote_copy(
        src_ref=src,
        dst_ref=dst,
        send_sem=send_sem,
        recv_sem=recv_sem,
        device_id=peer,
        device_id_type=MESH,
    )
    copy.start()
    return copy


def halo_peers(row, col, num_blk, num_hops, sign):
    return [
        (lax.rem(row + sign * hop(index) + num_blk, num_blk), col) for index in range(num_hops)
    ]


def pack_kernel(
    send_ref, dst_ref, src_ref, feat_ref, out_ref, local_ref, tile_of, prev_ref, last_ref, slot_dst
):
    slots, piece, side = out_ref.shape[1:]
    cap = send_ref.shape[2]
    blocks = last_ref.shape[0]
    locals_ = local_ref.shape[0]
    for slot in range(slots):
        start = pl.multiple_of(send_ref[0, slot // cap, slot % cap] * side, side)
        picked = feat_ref[:, pl.ds(start, side)]
        out_ref[0, slot] = picked[:piece]
        out_ref[1, slot] = picked[piece:]
    for at in range(locals_):
        start = pl.multiple_of(src_ref[slots + at] * side, side)
        local_ref[at] = feat_ref[:, pl.ds(start, side)]
    for block in range(blocks):
        last_ref[block] = 0

    def link(at, dst):
        prev_ref[at] = last_ref[dst]
        last_ref[dst] = at + 1

    def local_step(at, carry):
        link(at, dst_ref[slots + at])
        return carry

    def find_step(tile, carry):
        tile_of[src_ref[tile] - blocks] = tile
        return carry

    def slot_step(slot, carry):
        dst = dst_ref[tile_of[slot]]
        slot_dst[slot] = dst
        link(locals_ + slot, dst)
        return carry

    lax.fori_loop(0, locals_, local_step, 0)
    lax.fori_loop(0, slots, find_step, 0)
    lax.fori_loop(0, slots, slot_step, 0)


def gather_kernel(
    num_blk, num_col, tile_of, prev_ref, last_ref, sbuf, local_ref, feat_ref, cot_ref, cnt_hbm,
    feat_all, cot_all, all_a, all_b, floor_ref, half_ref,
    recv, sum_a, sum_b, sum_d, agg_src, cnt_ref,
    halo_send, halo_recv, col_send, col_recv, own_sem, cnt_sem,
):
    slots, piece, side = sbuf.shape[1:]
    num_hops = halo_send.shape[1]
    cap = slots // num_hops
    part = feat_all.shape[2]
    dim = 2 * piece
    locals_ = local_ref.shape[0]
    blocks = last_ref.shape[0]
    per_part = part // side
    row, col, col_peer = positions(num_blk, num_col)
    halo = halo_peers(row, col, num_blk, num_hops, 1)
    counts_in = pltpu.make_async_copy(cnt_hbm, cnt_ref, cnt_sem)
    counts_in.start()
    greet(halo + col_peer)
    halves = []
    for index in range(2):
        copies = []
        for at in range(num_hops):
            some = pl.ds(at * cap, cap)
            copies.append(
                push(
                    sbuf.at[index, some], recv.at[index, some], halo_send.at[index, at],
                    halo_recv.at[index, at], halo[at],
                )
            )
        halves.append(copies)
    later = []

    def share(at, pick, target):
        for step, peer in enumerate(col_peer):
            later.append(push(pick(peer[1]), target.at[col], col_send.at[at, step], col_recv.at[at, step], peer))
        own = pltpu.make_async_copy(pick(col), target.at[col], own_sem.at[at])
        own.start()
        later.append(own)

    def nodes_of(source):
        return lambda index: source.at[:, pl.ds(pl.multiple_of(index * part, part), part)]

    share(0, nodes_of(feat_ref), feat_all)
    share(1, nodes_of(cot_ref), cot_all)
    ones = jnp.ones((16, side), jnp.bfloat16)
    for total in (sum_a, sum_b, sum_d):
        total[0] = jnp.zeros(total.shape[1:], jnp.float32)
    counts_in.wait()

    def times(left, counts):
        return lax.dot_general(left, counts, (((1,), (1,)), ((), ())), preferred_element_type=jnp.float32)

    def local_step(at, carry):
        counts = cnt_ref[slots + at].astype(jnp.float32).astype(jnp.bfloat16)
        half_ref[slots + at] = counts
        product = times(jnp.concatenate([local_ref[at], ones], axis=0), counts)
        before = prev_ref[at]
        sum_a[at + 1] = sum_a[before] + product[:piece]
        sum_b[at + 1] = sum_b[before] + product[piece:dim]
        sum_d[at + 1] = sum_d[before] + product[dim:]
        return carry

    def first_step(slot, carry):
        counts = cnt_ref[tile_of[slot]].astype(jnp.float32).astype(jnp.bfloat16)
        half_ref[slot] = counts
        product = times(jnp.concatenate([recv[0, slot], ones], axis=0), counts)
        before = prev_ref[locals_ + slot]
        sum_a[locals_ + slot + 1] = sum_a[before] + product[:piece]
        sum_d[locals_ + slot + 1] = sum_d[before] + product[piece:]
        return carry

    def second_step(slot, carry):
        before = prev_ref[locals_ + slot]
        sum_b[locals_ + slot + 1] = sum_b[before] + times(recv[1, slot], half_ref[slot])
        return carry

    lax.fori_loop(0, locals_, local_step, 0, unroll=4)
    for index, (step, total, target) in enumerate(
        ((first_step, sum_a, all_a), (second_step, sum_b, all_b))
    ):
        for at, copy in enumerate(halves[index]):
            copy.wait()
            lax.fori_loop(at * cap, (at + 1) * cap, step, 0, unroll=True)
        for block in range(blocks):
            last = last_ref[block]
            group, left = block // per_part, (block % per_part) * side
            floor = jnp.maximum(sum_d[last][0:1], 1.0)
            if index == 0:
                floor_ref[group, :, left : left + side] = floor
            agg_src[index, group, :, left : left + side] = (total[last] / floor).astype(jnp.bfloat16)
        share(2 + index, lambda where: agg_src.at[index, where], target)
    for copy in later:
        copy.wait()


def dense_kernel(
    chunk, feat_ref, agg_a, agg_b, cot_ref, floor_ref, ws_ref, wn_ref, bias_ref,
    *outs,
):
    scaled_refs, (self_ref, grad_ref, acc) = outs[:-3], outs[-3:]
    width, nodes = feat_ref.shape
    parts, _, piece, side = scaled_refs[0].shape
    dim = self_ref.shape[1]
    col = lax.axis_index("col")
    self_weight, neigh_weight = ws_ref[...], wn_ref[...]
    first = (((0,), (0,)), ((), ()))
    last = (((1,), (1,)), ((), ()))
    bias = jnp.transpose(jnp.broadcast_to(bias_ref[...], (8, width)))[:, 0:1]
    for start in range(0, nodes, chunk):
        at = slice(start, start + chunk)
        feat = feat_ref[:, at]
        agg = jnp.concatenate(
            [half[part, :, at] for part in range(parts) for half in (agg_a, agg_b)], axis=0
        )
        pre_act = (
            lax.dot_general(self_weight, feat, first, preferred_element_type=jnp.float32)
            + lax.dot_general(neigh_weight, agg, first, preferred_element_type=jnp.float32)
            + bias
        )
        dz = (cot_ref[:, at].astype(jnp.float32) * gelu_slope(pre_act)).astype(jnp.bfloat16)
        floor = floor_ref[col, :, at]
        neigh = jnp.dot(neigh_weight, dz, preferred_element_type=jnp.float32) / floor
        own = jnp.dot(self_weight, dz, preferred_element_type=jnp.float32)
        for part in range(parts):
            rows = slice(part * dim, (part + 1) * dim)
            for index, scaled_ref in enumerate(scaled_refs):
                top = part * dim + index * piece
                for left in range(0, chunk, side):
                    scaled_ref[part, (start + left) // side] = neigh[
                        top : top + piece, left : left + side
                    ].astype(jnp.bfloat16)
            self_ref[part, :, at] = own[rows].astype(jnp.bfloat16)
        ones = jnp.ones((16, chunk), jnp.bfloat16)
        left = jnp.concatenate([feat, agg, ones], axis=0)
        grads = lax.dot_general(left, dz, last, preferred_element_type=jnp.float32)
        if start == 0:
            acc[...] = grads
        else:
            acc[...] += grads
    for part in range(parts):
        rows = slice(part * dim, (part + 1) * dim)
        grad_ref[part, :dim, :width] = acc[rows, :].astype(jnp.bfloat16)
        grad_ref[part, dim:, :width] = acc[width + part * dim : width + (part + 1) * dim, :].astype(
            jnp.bfloat16
        )
        bias_row = acc[2 * width : 2 * width + 1, rows].astype(jnp.bfloat16)
        grad_ref[part, :, width : width + dim] = jnp.broadcast_to(bias_row, (2 * dim, dim))
        if dim < grad_ref.shape[2] - width:
            rest = grad_ref.shape[2] - width - dim
            grad_ref[part, :, width + dim :] = jnp.zeros((2 * dim, rest), jnp.bfloat16)


def return_kernel(
    num_blk, num_col, slot_dst, half_ref, scaled_a, scaled_b, self_ref, grad_ref,
    all_a, all_b, came_ref, self_all, grad_out, bias_out,
    ret, core_buf, mid_src, mid_buf, far_src, far_buf, side_src, side_buf,
    halo_send, halo_recv, col_send, col_recv, core_send, core_recv, mid_send, mid_recv,
    far_send, far_recv, down_send, down_recv, own_sem,
):
    slots = ret.shape[1]
    num_hops = halo_send.shape[1]
    cap = slots // num_hops
    blocks = scaled_a.shape[1]
    row, col, col_peer = positions(num_blk, num_col)
    far_size = num_blk // 4
    core, mid, far = row % 2, (row // 2) % 2, row // 4
    width = grad_out.shape[4]
    halo = halo_peers(row, col, num_blk, num_hops, -1)
    core_peer = (far * 4 + mid * 2 + 1 - core, col)
    mid_peer = (far * 4 + (1 - mid) * 2 + core, col)
    far_peers = [((far + step) % far_size * 4 + mid * 2 + core, col) for step in range(1, far_size)]
    cross_peer = (far * 4 + (1 - mid) * 2 + 1 - core, col)
    greet(halo + [core_peer, mid_peer, cross_peer] + far_peers + col_peer)

    def across(at, source, target):
        return [
            push(source.at[peer[1]], target(step), col_send.at[at, step], col_recv.at[at, step], peer)
            for step, peer in enumerate(col_peer)
        ]

    def settle(copies):
        for copy in copies:
            copy.wait()

    mine = pl.ds(col * blocks, blocks)
    owns = []
    for at, (source, target) in enumerate(
        ((scaled_a.at[col], all_a.at[mine]), (scaled_b.at[col], all_b.at[mine]), (self_ref.at[col], self_all.at[col]))
    ):
        own = pltpu.make_async_copy(source, target, own_sem.at[at])
        own.start()
        owns.append(own)
    first = across(1, scaled_a, lambda step: all_a.at[mine])
    ups = [
        push(grad_ref.at[part, 1 - core], core_buf.at[part], core_send.at[part], core_recv.at[part], core_peer)
        for part in range(num_col)
    ]

    def spread(index, source):
        def body(slot, carry):
            picked = source[slot_dst[slot]]
            ret[index, slot] = jnp.dot(
                picked, half_ref[slot], preferred_element_type=jnp.float32
            ).astype(jnp.bfloat16)
            return carry

        lax.fori_loop(0, slots, body, 0, unroll=8)

    def give(index):
        copies = []
        for at in range(num_hops):
            part = pl.ds(at * cap, cap)
            copies.append(
                push(
                    ret.at[index, part], came_ref.at[index, part], halo_send.at[index, at],
                    halo_recv.at[index, at], halo[at],
                )
            )
        return copies

    settle(ups)
    for part in range(num_col):
        mid_src[part] = added(grad_ref[part, core], core_buf[part]).astype(jnp.bfloat16)
    ups = [
        push(mid_src.at[part, 1 - mid], mid_buf.at[part], mid_send.at[part], mid_recv.at[part], mid_peer)
        for part in range(num_col)
    ]
    settle(first)
    second = across(2, scaled_b, lambda step: all_b.at[mine])
    owns[0].wait()
    spread(0, all_a)
    settle(ups)
    for part in range(num_col):
        far_src[:, part] = added(mid_src[part, mid], mid_buf[part]).astype(jnp.bfloat16)
    ups = [
        push(far_src.at[peer[0] // 4], far_buf.at[step], far_send.at[step], far_recv.at[step], peer)
        for step, peer in enumerate(far_peers)
    ]
    later = give(0)
    settle(second)
    owns[1].wait()
    spread(1, all_b)
    settle(ups)
    total = far_src[far].astype(jnp.float32)
    for step in range(far_size - 1):
        total += far_buf[step].astype(jnp.float32)
    side_src[...] = total.astype(jnp.bfloat16)
    ups = across(0, side_src, lambda step: side_buf.at[step])
    later += across(3, self_ref, lambda step: self_all.at[col])
    settle(ups)
    total = side_src[col].astype(jnp.float32)
    for step in range(num_col - 1):
        total += side_buf[step].astype(jnp.float32)
    bias_out[...] = total[0:1, width:]
    grad_out[core, mid, far] = total[:, :width].astype(jnp.bfloat16)
    downs = [
        push(
            grad_out.at[core, mid, far], grad_out.at[core, mid, far], down_send.at[3 + step],
            down_recv.at[3 + step], peer,
        )
        for step, peer in enumerate(far_peers)
    ]
    later += give(1)
    settle(downs)
    settle([
        push(grad_out.at[core, mid], grad_out.at[core, mid], down_send.at[at], down_recv.at[at], peer)
        for at, peer in enumerate((core_peer, mid_peer, cross_peer))
    ])
    settle(later)
    owns[2].wait()


def finish_kernel(
    slots, send_ref, dst_ref, src_ref, half_ref, all_a, all_b, self_ref, came_ref, grad_ref, bias_ref,
    out_ref, grad_self, grad_neigh, grad_bias, acc,
):
    blocks, _, side = acc.shape
    num_hops, cap = send_ref.shape[1:]
    piece = all_a.shape[1]
    dim = grad_self.shape[0]
    grad_self[...] = grad_ref[:dim].astype(jnp.float32)
    grad_neigh[...] = grad_ref[dim:].astype(jnp.float32)
    grad_bias[...] = bias_ref[:, :dim]
    acc[...] = jnp.zeros_like(acc)
    for tile in range(slots, dst_ref.shape[0]):
        dst = dst_ref[tile]
        picked = jnp.concatenate([all_a[dst], all_b[dst]], axis=0)
        acc[src_ref[tile]] += jnp.dot(picked, half_ref[tile], preferred_element_type=jnp.float32)
    for slot in range(slots):
        came = jnp.concatenate([came_ref[0, slot], came_ref[1, slot]], axis=0)
        acc[send_ref[0, slot // cap, slot % cap]] += came.astype(jnp.float32)
    per_part = self_ref.shape[2] // side
    for block in range(blocks):
        at = (block % per_part) * side
        own = self_ref[block // per_part, :, at : at + side].astype(jnp.float32)
        out_ref[:, block * side : (block + 1) * side] = (acc[block] + own).astype(jnp.bfloat16)


def per_device(
    num_blk, num_col,
    node_feats, tile_dst, tile_src, tile_cnt, send_blk, self_weight, neigh_weight, bias, cotangent,
):
    half, full = jnp.bfloat16, jnp.float32
    dim, rows = node_feats.shape
    tiles, side, _ = tile_cnt.shape
    blocks = rows // side
    num_hops, cap = send_blk.shape[1:]
    slots = num_hops * cap
    part = rows // num_col
    width = self_weight.shape[0]
    dma = pltpu.SemaphoreType.DMA
    shape = jax.ShapeDtypeStruct
    peers = max(num_col - 1, 1)
    split = shape((num_col, dim, part), half)
    locals_ = tiles - slots
    piece = dim // 2
    slot_shape = shape((2, slots, piece, side), half)
    ints = lambda count: shape((count,), jnp.int32)

    outgoing, local_src, tile_of, prev, last, slot_dst = pl.pallas_call(
        pack_kernel,
        out_shape=(
            slot_shape, shape((locals_, dim, side), half), ints(slots), ints(tiles), ints(blocks), ints(slots),
        ),
        in_specs=[smem()] * 3 + [vmem()],
        out_specs=(vmem(), vmem()) + (smem(),) * 4,
        compiler_params=params(),
        name="pack",
    )(send_blk, tile_dst, tile_src, node_feats)
    agg_shape = shape((num_col, piece, part), half)
    hbm = pl.BlockSpec(memory_space=pltpu.HBM)
    sums = lambda count: pltpu.VMEM((tiles + 1, count, side), full)
    feat_all, cot_all, agg_a, agg_b, floor, half_cnt = pl.pallas_call(
        functools.partial(gather_kernel, num_blk, num_col),
        out_shape=(
            split, split, agg_shape, agg_shape, shape((num_col, 1, part), full), shape((tiles, side, side), half),
        ),
        in_specs=[smem()] * 3 + [vmem()] * 2 + [hbm] * 3,
        out_specs=(vmem(),) * 6,
        scratch_shapes=[
            pltpu.VMEM(slot_shape.shape, half), sums(piece), sums(piece), sums(16),
            pltpu.VMEM((2, num_col, piece, part), half), pltpu.VMEM((tiles, side, side), jnp.int32),
            dma((2, num_hops)), dma((2, num_hops)), dma((4, peers)), dma((4, peers)), dma((4,)), dma(()),
        ],
        compiler_params=params(0, 24 * 1024 * 1024),
        name="gather",
    )(tile_of, prev, last, outgoing, local_src, node_feats, cotangent, tile_cnt)

    lanes = width + 128
    per_part = part // side
    scaled_shape = shape((num_col, per_part, piece, side), half)
    scaled_a, scaled_b, own_part, grads = pl.pallas_call(
        functools.partial(dense_kernel, min(part, 256)),
        out_shape=(scaled_shape, scaled_shape, split, shape((num_col, 2 * dim, lanes), half)),
        in_specs=[vmem()] * 8,
        out_specs=(vmem(),) * 4,
        scratch_shapes=[pltpu.VMEM((2 * width + 16, width), full)],
        compiler_params=params(),
        name="dense",
    )(
        feat_all.reshape(width, part), agg_a, agg_b, cot_all.reshape(width, part),
        floor, self_weight, neigh_weight, bias.reshape(1, width),
    )

    far_size = num_blk // 4
    span = 2 * dim // num_blk
    all_shape = shape((blocks, piece, side), half)
    level = lambda *lead: pltpu.VMEM(lead + (span, lanes), half)
    all_a, all_b, came, own_all, grad_sum, bias_sum = pl.pallas_call(
        functools.partial(return_kernel, num_blk, num_col),
        out_shape=(
            all_shape, all_shape, shape((2, slots, piece, side), half), split,
            shape((2, 2, far_size, span, width), half), shape((1, 128), full),
        ),
        in_specs=[smem()] + [vmem()] * 5,
        out_specs=(vmem(),) * 6,
        scratch_shapes=[
            pltpu.VMEM((2, slots, piece, side), half),
            level(num_col, 2, far_size), level(num_col, 2, far_size), level(num_col, far_size),
            level(far_size, num_col), level(max(far_size - 1, 1), num_col), level(num_col), level(peers),
            dma((2, num_hops)), dma((2, num_hops)), dma((4, peers)), dma((4, peers)),
            dma((num_col,)), dma((num_col,)), dma((num_col,)), dma((num_col,)),
            dma((far_size,)), dma((far_size,)), dma((far_size + 2,)), dma((far_size + 2,)),
            dma((3,)),
        ],
        compiler_params=params(2),
        name="give_back",
    )(
        slot_dst, half_cnt, scaled_a, scaled_b, own_part,
        grads.reshape(num_col, 2, 2, far_size, span, lanes),
    )

    weight_shape = shape((dim, width), full)
    grad_feats, grad_self, grad_neigh, grad_bias = pl.pallas_call(
        functools.partial(finish_kernel, slots),
        out_shape=(shape((dim, rows), half), weight_shape, weight_shape, shape((1, dim), full)),
        in_specs=[smem()] * 3 + [vmem()] * 7,
        out_specs=(vmem(),) * 4,
        scratch_shapes=[pltpu.VMEM((blocks, dim, side), full)],
        compiler_params=params(),
        name="finish",
    )(
        send_blk, tile_dst, tile_src, half_cnt, all_a, all_b, own_all, came,
        grad_sum.reshape(2 * dim, width), bias_sum,
    )
    return (grad_feats, grad_self, grad_neigh, grad_bias.reshape(dim))


def solution(mesh):
    placed = (
        P("col", "blk"),
        P("blk"),
        P("blk"),
        P("blk", None, None),
        P("blk", None, None),
        P(),
        P(),
        P(),
        P("col", "blk"),
    )
    return jax.shard_map(
        functools.partial(per_device, mesh.shape["blk"], mesh.shape["col"]),
        mesh=mesh,
        in_specs=placed,
        out_specs=(P("col", "blk"), P("col", None), P("col", None), P("col")),
        check_vma=False,
    )
```
